256 devices in a mesh: row: 16 (over y, x), col: 8 (over z), depth: 2 (over core).
Axes of the slice: x: 4, y: 4, z: 8, core: 2. Of those that a mesh axis runs over, the one named last changes fastest.
Arguments:
- t_amps: bfloat16 [800, 400, 400], P(('col', 'depth'), 'row'), may hold values from -6 to 6
- integrals: bfloat16 [400, 400, 6400], P('row', None, ('col', 'depth')), may hold values from -0.0390625 to 0.0390625
- virt_irrep: int32 [400], replicated, may hold values from 0 to 7, as said below
- tile_map: int32 [16, 16], replicated, may hold values 0 or 1
Outputs:
- ladder: bfloat16 [800, 6400], P('row', ('col', 'depth'))
The draws below stay inside these ranges and needn't reach their ends.
Inputs may be any that keep to these rules, and one draw needn't show every extreme that they name: `virt_irrep`: nondecreasing; the first label is 0 and the last is 7.
All inputs are finite; a program needn't handle non-finite values.
Results may differ from the reference program's by a relative error of at most 0.0051.
Values may be sent and summed in bfloat16 or wider, within the bound.
No kernel may reach another device: no remote copies, remote signals or barrier semaphores. Data moves between devices by JAX's collectives and lax.ppermute only.
A program may use at most 128 MiB of HBM per device.

```python
import jax
import jax.numpy as jnp
from jax import lax

NVIR = 400
A_WIN = 16
TILE = 25
PAIRS = 800
COLS = 6400


def draw_virt_irrep(key, part):
    key = jax.random.fold_in(key, 23)
    labels = jnp.sort(jax.random.randint(key, (NVIR,), 0, 8, dtype=jnp.int32))
    return labels.at[0].set(0).at[NVIR - 1].set(7)


def plant(result, rng, low, largest):
    index_at = [jax.random.randint(jax.random.fold_in(rng, axis), (), 0, length) for axis, length in enumerate(result.shape)]
    main_axis = result.shape.index(max(result.shape))
    neighbour = index_at[:main_axis] + [(index_at[main_axis] + 1) % result.shape[main_axis]] + index_at[main_axis + 1:]
    return result.at[tuple(index_at)].set(low).at[tuple(neighbour)].set(largest)


def block_scale(key, shape, pieces, low, largest):
    loudness = 1.0
    for position, blocks in pieces:
        steps = jax.random.uniform(jax.random.fold_in(jax.random.fold_in(key, 6), position), (blocks,), jnp.float32, low / len(pieces), largest / len(pieces))
        loudness = loudness * jnp.repeat(jnp.exp(steps), shape[position] // blocks).reshape((-1,) + (1,) * (len(shape) - 1 - position))
    return loudness


def scatter_about(rng, extent, spread, bound, shards=(), kind=jnp.bfloat16):
    drawn = spread * jax.random.normal(rng, extent, jnp.float32)
    if shards:
        drawn = drawn * block_scale(rng, extent, shards, -0.22, 0.18)
    return jnp.clip(drawn, -bound, bound).astype(kind)


def setup_inputs(seed: int = 0) -> dict:
    seeds = jax.random.split(jax.random.key(seed), 5)
    t_amps = scatter_about(seeds[0], (PAIRS, NVIR, NVIR), 1.0, 6.0, ((0, 16), (1, 16)))
    integrals = scatter_about(seeds[1], (NVIR, NVIR, COLS), (NVIR * NVIR // 8) ** -0.5, 0.0390625, ((0, 16), (2, 16)))
    virt_irrep = draw_virt_irrep(jax.random.fold_in(seeds[4], 71), 0)
    tile_map = plant((jax.random.randint(seeds[3], (NVIR // TILE, NVIR // TILE), 0, 4) < 3).astype(jnp.int32), jax.random.fold_in(seeds[3], 1), 0, 1)
    return {"t_amps": t_amps, "integrals": integrals, "virt_irrep": virt_irrep, "tile_map": tile_map}


def reference(t_amps, integrals, virt_irrep, tile_map):
    diff = t_amps.astype(jnp.float32) - jnp.transpose(t_amps, (0, 2, 1)).astype(jnp.float32)
    anti = diff.astype(jnp.bfloat16).reshape(PAIRS, NVIR * NVIR)
    kept = jnp.repeat(jnp.repeat(tile_map, TILE, axis=0), TILE, axis=1) != 0
    cd_irrep = jnp.bitwise_xor(virt_irrep[:, None], virt_irrep[None, :])

    def one_slab(index):
        block = lax.dynamic_slice_in_dim(integrals, (index * NVIR).astype(jnp.int32), NVIR, 2)
        ab_irrep = jnp.bitwise_xor(virt_irrep[index], virt_irrep)
        allowed = kept[:, :, None] & (jnp.bitwise_xor(cd_irrep[:, :, None], ab_irrep[None, None, :]) == 0)
        masked = jnp.where(allowed, block, jnp.zeros((), block.dtype)).reshape(NVIR * NVIR, NVIR)
        return 0.5 * jnp.dot(anti, masked, preferred_element_type=jnp.float32)

    slabs = lax.map(one_slab, jnp.arange(A_WIN, dtype=jnp.int32))
    return jnp.transpose(slabs, (1, 0, 2)).reshape(PAIRS, COLS).astype(jnp.bfloat16)
```

```python
import jax
import jax.numpy as jnp
import numpy as np
from jax import lax
from jax.experimental import pallas as pl
from jax.experimental.pallas import tpu as pltpu
from jax.sharding import PartitionSpec as P

TILE = 25
LANES = 128
WINDOW = 16
SIDE = 4
WHOLE = ((3, 2), (2, 1), (3, 3), (1, 3), (0, 1), (1, 0))
SPLIT = ((0, 2), (2, 0), (2, 2), (0, 0))
NOWHERE = -(1 << 20)
VMEM_BYTES = 52 * 1024 * 1024


def split_pairs(variant):
    chosen = [(u, v) for u in range(TILE) for v in range(u + 1, TILE)]
    middle = (TILE + 1) // 2
    if variant == 0:
        chosen += [(u, u) for u in range(middle)]
    elif variant == 1:
        chosen += [(u, u) for u in range(middle, TILE)]
    return chosen


def whole_pairs():
    return [(u, v) for u in range(TILE) for v in range(TILE)]


def padded_flat(count):
    return -(-count // LANES) * LANES


def row_targets(pairs, rows, swapped):
    target = np.full((rows, 1), NOWHERE, np.int32)
    for k, (u, v) in enumerate(pairs):
        target[k, 0] = v * 3 * WINDOW + u if swapped else u * 3 * WINDOW + v
    return target


def swap_row(flat):
    row = np.full((1, flat), NOWHERE, np.int32)
    for u, v in whole_pairs():
        row[0, v * TILE + u] = u * TILE + v
    return jnp.asarray(row)


def choice_rows(flat):
    rows = np.full((3, 1, flat // 2), NOWHERE, np.int32)
    for variant in range(3):
        for k, (u, v) in enumerate(split_pairs(variant)):
            rows[variant, 0, k] = u * TILE + v
    return jnp.asarray(rows)


def one_hot(row, count, dtype):
    places = lax.broadcasted_iota(jnp.int32, (count, row.shape[1]), 0)
    return jnp.where(places == row, 1.0, 0.0).astype(dtype)


def neighbour(row, offset, sign):
    y = (row // SIDE + sign * offset[0]) % SIDE
    x = (row % SIDE + sign * offset[1]) % SIDE
    return y * SIDE + x


def schedule(sign):
    others = np.zeros((SIDE * SIDE, len(WHOLE) + len(SPLIT)), np.int32)
    variants = np.zeros_like(others)
    for row in range(SIDE * SIDE):
        for k, offset in enumerate(WHOLE + SPLIT):
            other = neighbour(row, offset, sign)
            worker, source = (row, other) if sign == 1 else (other, row)
            others[row, k] = other
            variants[row, k] = 2 if offset == (0, 0) else int(worker > source)
    return jnp.asarray(others.ravel()), jnp.asarray(variants.ravel())


def antisymmetrize(own, mirrored, place, body_rows):
    tiles, pairs, flat = own.shape
    whole, split = len(WHOLE), len(SPLIT)
    slots = whole + split // 2
    left = pairs - body_rows
    padded = -(-pairs // 16) * 16

    def body(place_ref, places_ref, variants_ref, own_ref, mirrored_ref, swap_ref, choice_ref, out, stack, rest, tile):
        first = place_ref[0] * (whole + split)
        for k in range(whole + split):
            stack[padded * k:padded * k + pairs] = mirrored_ref[places_ref[first + k]]
        swap = one_hot(swap_ref[...], flat, own.dtype)
        swapped = jnp.dot(stack[...], swap, preferred_element_type=jnp.float32)

        def difference(k):
            return own_ref[places_ref[first + k]].astype(jnp.float32) - swapped[padded * k:padded * k + pairs]

        def store(slot, value):
            out[body_rows * slot:body_rows * (slot + 1)] = value[:body_rows].astype(own.dtype)
            rest[left * slot:left * (slot + 1)] = value[body_rows:]

        for k in range(whole):
            store(k, difference(k))
        for m in range(split // 2):
            ends = []
            for k in (whole + 2 * m, whole + 2 * m + 1):
                tile[:pairs] = difference(k).astype(own.dtype)
                choice = one_hot(choice_ref[variants_ref[first + k]], flat, own.dtype)
                ends.append(jnp.dot(tile[...], choice, preferred_element_type=jnp.float32)[:pairs])
            store(whole + m, jnp.concatenate(ends, axis=1))
        out[body_rows * slots:] = rest[...].astype(own.dtype)

    smem = pl.BlockSpec(memory_space=pltpu.SMEM)
    vmem = pl.BlockSpec(memory_space=pltpu.VMEM)
    return pl.pallas_call(
        body,
        in_specs=[smem, smem, smem, vmem, vmem, vmem, vmem],
        out_shape=jax.ShapeDtypeStruct((slots * pairs, flat), own.dtype),
        scratch_shapes=[
            pltpu.VMEM(((whole + split) * padded, flat), own.dtype),
            pltpu.VMEM((left * slots, flat), jnp.float32),
            pltpu.VMEM((padded, flat), own.dtype),
        ],
        compiler_params=pltpu.CompilerParams(vmem_limit_bytes=VMEM_BYTES),
        name="antisymmetrize",
    )(place, *schedule(1), own, mirrored, swap_row(flat), choice_rows(flat))


def packed_rows(rows, cols):
    main, over = cols // LANES, cols % LANES
    per = LANES // over
    return main, over, per, -(-rows // per // 16) * 16


def take_tiles(integrals, place, irrep, tile_map, base, whole, split, swapped):
    c_count, virt, cols = integrals.shape
    flat = padded_flat(TILE * TILE)
    half = flat // 2
    blocks = virt // WINDOW
    span = 3 * WINDOW
    whole_target = jnp.asarray(row_targets(whole_pairs(), flat, swapped))
    split_target = jnp.asarray(np.stack([row_targets(split_pairs(v), half, swapped) for v in range(3)]))
    main, over, per, _ = packed_rows(flat, cols)
    sizes = [flat] * whole + [half] * split
    stripes = [max(-(-rows // per), 80) for rows in sizes]

    slots = len(WHOLE) + len(SPLIT)

    def body(place_ref, others_ref, variants_ref, irrep_ref, kept_ref,
             r0, r1, r2, column_ref, whole_ref, split_ref, v0, v1, v2, *refs):
        outs, slab = refs[:-1], refs[-1]
        s = pl.program_id(0)
        row, shard = place_ref[0], place_ref[1]
        entry = row * slots + base + s
        other = others_ref[entry]
        offset = other * TILE % WINDOW
        dropped = jnp.where(kept_ref[row, other] != 0, 0, 1 << 20)
        for q, (r, v) in enumerate(((r0, v0), (r1, v1), (r2, v2))):
            code = jnp.bitwise_xor(r[...], column_ref[...])
            for c in range(c_count):
                wanted = jnp.bitwise_xor(irrep_ref[row * c_count + c], irrep_ref[shard]) + dropped
                kept = jnp.where(code == wanted, v[c].astype(jnp.float32), 0.0)
                slab[span * c + WINDOW * q:span * c + WINDOW * (q + 1), :] = kept.astype(integrals.dtype)

        def pick(target):
            place = lax.broadcasted_iota(jnp.int32, (target.shape[0], span * c_count), 1)
            chosen = jnp.where(place == target + offset, 1.0, 0.0).astype(integrals.dtype)
            return jnp.dot(chosen, slab[...], preferred_element_type=jnp.float32).astype(integrals.dtype)

        def pack(out, rows, stripe, value):
            for b in range(main):
                out[rows * b:rows * (b + 1), :] = value[:, LANES * b:LANES * (b + 1)]
            strips = [value[stripe * i:stripe * (i + 1), LANES * main:] for i in range(rows // stripe)]
            strips += [jnp.zeros_like(strips[0])] * (per - len(strips))
            out[rows * main:, :] = jnp.concatenate(strips, axis=1)

        @pl.when(s < whole)
        def _():
            value = pick(whole_ref[...])
            if swapped:
                for k in range(whole):
                    @pl.when(s == k)
                    def _(k=k):
                        pack(outs[k], flat, stripes[k], value)
            else:
                outs[0][0] = value

        @pl.when(s >= whole)
        def _():
            value = pick(split_ref[variants_ref[entry]])
            for k in range(whole, whole + split):
                @pl.when(s == k)
                def _(k=k):
                    if swapped:
                        pack(outs[k], half, stripes[k], value)
                    else:
                        low = half * ((k - whole) % 2)
                        outs[0][0, low:low + half, :] = value

    def block(q, s, place, others):
        start = others[place[0] * slots + base + s] * TILE
        return jnp.minimum(start // WINDOW + q, blocks - 1)

    def window(q):
        return lambda s, place, others, *_: (0, block(q, s, place, others), 0)

    def code_window(q):
        return lambda s, place, others, *_: (block(q, s, place, others), 0)

    fixed = lambda rank: (lambda s, *_: (0,) * rank)
    if swapped:
        shapes = [(main * rows + stripe, LANES) for rows, stripe in zip(sizes, stripes)]
        out_specs = [pl.BlockSpec(shape, fixed(2)) for shape in shapes]
        out_shape = [jax.ShapeDtypeStruct(shape, integrals.dtype) for shape in shapes]
    else:
        out_specs = [pl.BlockSpec(
            (1, flat, cols), lambda s, *_: (jnp.where(s < whole, s, whole + (s - whole) // 2), 0, 0))]
        out_shape = [jax.ShapeDtypeStruct((whole + split // 2, flat, cols), integrals.dtype)]
    return pl.pallas_call(
        body,
        grid_spec=pltpu.PrefetchScalarGridSpec(
            num_scalar_prefetch=5,
            grid=(whole + split,),
            in_specs=[pl.BlockSpec((WINDOW, 1), code_window(q)) for q in range(3)]
            + [
                pl.BlockSpec((1, cols), fixed(2)),
                pl.BlockSpec((flat, 1), fixed(2)),
                pl.BlockSpec((3, half, 1), fixed(3)),
            ]
            + [pl.BlockSpec((c_count, WINDOW, cols), window(q)) for q in range(3)],
            out_specs=out_specs,
            scratch_shapes=[pltpu.VMEM((span * c_count, cols), integrals.dtype)],
        ),
        out_shape=out_shape,
        compiler_params=pltpu.CompilerParams(vmem_limit_bytes=VMEM_BYTES),
        cost_estimate=pl.CostEstimate(
            flops=2 * (whole + split // 2) * flat * span * c_count * cols,
            bytes_accessed=2 * (whole + split) * span * c_count * cols, transcendentals=0),
        name="take_swapped_tiles" if swapped else "take_own_tiles",
    )(place, *schedule(-1 if swapped else 1), irrep, tile_map, *[irrep[:, None]] * 3, irrep[None, :],
      whole_target, split_target, integrals, integrals, integrals)


def tile_major(t):
    c_count, pairs, virt = t.shape
    tiles = virt // TILE
    flat = -(-c_count * TILE // LANES) * LANES

    def body(t_ref, out_ref):
        for j in range(tiles):
            parts = [t_ref[c, :, TILE * j:TILE * (j + 1)] for c in range(c_count)]
            parts.append(jnp.zeros((pairs, flat - c_count * TILE), t.dtype))
            out_ref[j] = jnp.concatenate(parts, axis=1)

    return pl.pallas_call(
        body,
        out_shape=jax.ShapeDtypeStruct((tiles, pairs, flat), t.dtype),
        compiler_params=pltpu.CompilerParams(vmem_limit_bytes=VMEM_BYTES),
        name="tile_major",
    )(t)


def contract(gathered, held, others, body_rows):
    shards, rows, flat = gathered.shape
    slots, _, cols = held.shape
    pairs = rows // slots
    left = pairs - body_rows
    rest_rows = left * slots
    whole = len(WHOLE)
    half = flat // 2
    main, over, per, _ = packed_rows(flat, cols)
    strip = body_rows // per
    tail_rows = padded_tail(body_rows, left, cols)

    def body(main_ref, rest_ref, held_ref, *refs):
        others_ref, (out, weights, left_side, spread, rests, sums, tail) = refs[:-7], refs[-7:]
        slot = pl.program_id(0)

        def less(low, count, other):
            stripe = other.shape[0] - main * count
            for b in range(main):
                lanes = slice(LANES * b, LANES * (b + 1))
                weights[low:low + count, lanes] = (
                    held_ref[0, low:low + count, lanes].astype(jnp.float32)
                    - other[count * b:count * (b + 1), :].astype(jnp.float32)
                ).astype(held.dtype)
            last = other[count * main:, :].astype(jnp.float32)
            for i in range(count // stripe):
                at = slice(low + stripe * i, low + stripe * (i + 1))
                weights[at, LANES * main:] = (
                    held_ref[0, at, LANES * main:].astype(jnp.float32) - last[:, over * i:over * (i + 1)]
                ).astype(held.dtype)

        for k in range(slots):
            @pl.when(slot == k)
            def _(k=k):
                if k < whole:
                    less(0, flat, others_ref[k])
                else:
                    less(0, half, others_ref[whole + 2 * (k - whole)])
                    less(half, half, others_ref[whole + 2 * (k - whole) + 1])

        @pl.when(slot == 0)
        def _():
            sums[...] = jnp.zeros(sums.shape, jnp.float32)
            for b in range(flat // LANES):
                lanes = slice(LANES * b, LANES * (b + 1))
                spread[...] = rest_ref[:, :, lanes].reshape(shards * rest_rows, LANES).astype(jnp.float32)
                for k in range(slots):
                    rests[k, :, lanes] = jnp.concatenate([
                        spread[pl.ds(left * k + i, shards, stride=rest_rows), :] for i in range(left)
                    ], axis=0).astype(rests.dtype)

        left_side[:shards * body_rows] = main_ref[...].reshape(shards * body_rows, flat)
        left_side[shards * body_rows:] = rests[slot]
        sums[...] += jnp.dot(left_side[...], weights[...], preferred_element_type=jnp.float32)

        @pl.when(slot == slots - 1)
        def _():
            total = 0.5 * sums[...]
            full = total[:shards * body_rows].reshape(shards, body_rows, cols)
            folded = jnp.stack([
                total[shards * (body_rows + i):shards * (body_rows + i + 1)] for i in range(left)], axis=1)
            for b in range(main):
                lanes = slice(LANES * b, LANES * (b + 1))
                out[:, body_rows * b:body_rows * (b + 1), :] = full[:, :, lanes].astype(out.dtype)
                tail[:, left * b:left * (b + 1), :] = folded[:, :, lanes]
            at = left * main
            tail[:, at + strip + left:, :] = jnp.zeros((shards, tail_rows - at - strip - left, LANES), jnp.float32)
            for i in range(per):
                tail[:, at:at + strip, over * i:over * (i + 1)] = full[:, strip * i:strip * (i + 1), LANES * main:]
            tail[:, at + strip:at + strip + left, over:] = jnp.zeros((shards, left, LANES - over), jnp.float32)
            tail[:, at + strip:at + strip + left, :over] = folded[:, :, LANES * main:]
            out[:, body_rows * main:, :] = tail[...].astype(out.dtype)

    out_rows = body_rows * main + tail_rows
    return pl.pallas_call(
        body,
        grid=(slots,),
        in_specs=[
            pl.BlockSpec((shards, body_rows, flat), lambda k: (0, k, 0)),
            pl.BlockSpec((shards, rest_rows, flat), lambda k: (0, body_rows * slots // rest_rows, 0)),
            pl.BlockSpec((1, flat, cols), lambda k: (k, 0, 0)),
        ]
        + [pl.BlockSpec(memory_space=pltpu.VMEM) for other in others],
        out_specs=pl.BlockSpec((shards, out_rows, LANES), lambda k: (0, 0, 0)),
        out_shape=jax.ShapeDtypeStruct((shards, out_rows, LANES), gathered.dtype),
        scratch_shapes=[
            pltpu.VMEM((flat, cols), held.dtype),
            pltpu.VMEM((shards * pairs, flat), held.dtype),
            pltpu.VMEM((shards * rest_rows, LANES), jnp.float32),
            pltpu.VMEM((slots, shards * left, flat), held.dtype),
            pltpu.VMEM((shards * pairs, cols), jnp.float32),
            pltpu.VMEM((shards, tail_rows, LANES), jnp.float32),
        ],
        compiler_params=pltpu.CompilerParams(vmem_limit_bytes=VMEM_BYTES),
        cost_estimate=pl.CostEstimate(
            flops=2 * slots * shards * pairs * flat * cols,
            bytes_accessed=2 * gathered.size + 2 * held.size, transcendentals=0),
        name="contract",
    )(gathered, gathered, held, *others)


def padded_tail(body_rows, left, cols):
    main, over, per, _ = packed_rows(body_rows, cols)
    return -(-(left * main + body_rows // per + left) // 16) * 16


def add_pieces(pieces, body_rows, left, cols):
    main, over, per, _ = packed_rows(body_rows, cols)
    strip = body_rows // per

    def body(pieces_ref, out, scratch):
        total = jnp.sum(pieces_ref[...].astype(jnp.float32), axis=0)
        tail = total[body_rows * main:]
        at = left * main
        for b in range(main):
            lanes = slice(LANES * b, LANES * (b + 1))
            scratch[:body_rows, lanes] = total[body_rows * b:body_rows * (b + 1)]
            scratch[body_rows:, lanes] = tail[left * b:left * (b + 1)]
        for i in range(per):
            scratch[strip * i:strip * (i + 1), LANES * main:] = tail[at:at + strip, over * i:over * (i + 1)]
        scratch[body_rows:, LANES * main:] = tail[at + strip:at + strip + left, :over]
        out[...] = scratch[...].astype(out.dtype)

    return pl.pallas_call(
        body,
        out_shape=jax.ShapeDtypeStruct((body_rows + left, cols), pieces.dtype),
        scratch_shapes=[pltpu.VMEM((body_rows + left, cols), jnp.float32)],
        compiler_params=pltpu.CompilerParams(vmem_limit_bytes=VMEM_BYTES),
        name="add_pieces",
    )(pieces)


BODY_ROWS = 48
EARLY = 1


def local(t_amps, integrals, virt_irrep, tile_map):
    own_rows, c_count, virt_count = t_amps.shape
    own_cols = integrals.shape[2]
    assert c_count == TILE and own_cols == virt_count
    whole, split = len(WHOLE), len(SPLIT)
    place = jnp.stack([lax.axis_index("row"), lax.axis_index(("col", "depth"))]).astype(jnp.int32)

    own = tile_major(jnp.transpose(t_amps, (1, 0, 2)))
    mirrored = lax.all_to_all(own, "row", split_axis=0, concat_axis=0, tiled=True)
    sent_whole = take_tiles(integrals, place, virt_irrep, tile_map, 0, whole, 0, True)
    mirrored, sent_whole = lax.optimization_barrier((mirrored, sent_whole))
    part = antisymmetrize(own, mirrored, place, BODY_ROWS)
    part, sent_whole, place = lax.optimization_barrier((part, sent_whole, place))
    gathered = lax.all_gather(part, ("col", "depth"), axis=0, tiled=False)

    def exchange(offsets, tiles):
        moved = []
        for offset, tile in zip(offsets, tiles):
            if offset != (0, 0):
                moves = [(neighbour(r, offset, 1), r) for r in range(SIDE * SIDE)]
                tile = lax.ppermute(tile, "row", moves)
            moved.append(tile)
        return moved

    others = exchange(WHOLE, sent_whole)
    held = take_tiles(integrals, place, virt_irrep, tile_map, 0, whole, split, False)[0]
    held, place = lax.optimization_barrier((held, place))
    sent_split = take_tiles(integrals, place, virt_irrep, tile_map, whole, 0, split, True)
    others[:EARLY], sent_split = lax.optimization_barrier((others[:EARLY], sent_split))
    others = others + exchange(SPLIT, sent_split)
    result = contract(gathered, held, others, BODY_ROWS)
    pieces = lax.all_to_all(result, "row", split_axis=0, concat_axis=0, tiled=True)
    return add_pieces(pieces, BODY_ROWS, own_rows - BODY_ROWS, own_cols)


def solution(mesh):
    placed = (P(("col", "depth"), "row", None), P("row", None, ("col", "depth")), P(), P())
    return jax.shard_map(
        local, mesh=mesh, in_specs=placed, out_specs=P("row", ("col", "depth")), check_vma=False
    )
```

```python
import jax
import jax.numpy as jnp
import numpy as np
from jax import lax
from jax.experimental import pallas as pl
from jax.experimental.pallas import tpu as pltpu
from jax.sharding import PartitionSpec as P

TILE = 25
LANES = 128
WINDOW = 16
SIDE = 4
WHOLE = ((3, 2), (2, 1), (3, 3), (1, 3), (0, 1), (1, 0))
SPLIT = ((0, 2), (2, 0), (2, 2), (0, 0))
NOWHERE = -(1 << 20)
VMEM_BYTES = 52 * 1024 * 1024


def split_pairs(variant):
    chosen = [(u, v) for u in range(TILE) for v in range(u + 1, TILE)]
    middle = (TILE + 1) // 2
    if variant == 0:
        chosen += [(u, u) for u in range(middle)]
    elif variant == 1:
        chosen += [(u, u) for u in range(middle, TILE)]
    return chosen


def whole_pairs():
    return [(u, v) for u in range(TILE) for v in range(TILE)]


def padded_flat(count):
    return -(-count // LANES) * LANES


def row_targets(pairs, rows, swapped):
    target = np.full((rows, 1), NOWHERE, np.int32)
    for k, (u, v) in enumerate(pairs):
        target[k, 0] = v * 3 * WINDOW + u if swapped else u * 3 * WINDOW + v
    return target


def swap_row(flat):
    row = np.full((1, flat), NOWHERE, np.int32)
    for u, v in whole_pairs():
        row[0, v * TILE + u] = u * TILE + v
    return jnp.asarray(row)


def choice_rows(flat):
    rows = np.full((3, 1, flat // 2), NOWHERE, np.int32)
    for variant in range(3):
        for k, (u, v) in enumerate(split_pairs(variant)):
            rows[variant, 0, k] = u * TILE + v
    return jnp.asarray(rows)


def one_hot(row, count, dtype):
    places = lax.broadcasted_iota(jnp.int32, (count, row.shape[1]), 0)
    return jnp.where(places == row, 1.0, 0.0).astype(dtype)


def neighbour(row, offset, sign):
    y = (row // SIDE + sign * offset[0]) % SIDE
    x = (row % SIDE + sign * offset[1]) % SIDE
    return y * SIDE + x


def schedule(sign):
    others = np.zeros((SIDE * SIDE, len(WHOLE) + len(SPLIT)), np.int32)
    variants = np.zeros_like(others)
    for row in range(SIDE * SIDE):
        for k, offset in enumerate(WHOLE + SPLIT):
            other = neighbour(row, offset, sign)
            worker, source = (row, other) if sign == 1 else (other, row)
            others[row, k] = other
            variants[row, k] = 2 if offset == (0, 0) else int(worker > source)
    return jnp.asarray(others.ravel()), jnp.asarray(variants.ravel())


def antisymmetrize(own, mirrored, place, body_rows):
    tiles, pairs, flat = own.shape
    whole, split = len(WHOLE), len(SPLIT)
    slots = whole + split // 2
    left = pairs - body_rows
    padded = -(-pairs // 16) * 16

    def body(place_ref, places_ref, variants_ref, own_ref, mirrored_ref, swap_ref, choice_ref, out, stack, rest, tile):
        first = place_ref[0] * (whole + split)
        for k in range(whole + split):
            stack[padded * k:padded * k + pairs] = mirrored_ref[places_ref[first + k]]
        swap = one_hot(swap_ref[...], flat, own.dtype)
        swapped = jnp.dot(stack[...], swap, preferred_element_type=jnp.float32)

        def difference(k):
            return own_ref[places_ref[first + k]].astype(jnp.float32) - swapped[padded * k:padded * k + pairs]

        def store(slot, value):
            out[body_rows * slot:body_rows * (slot + 1)] = value[:body_rows].astype(own.dtype)
            rest[left * slot:left * (slot + 1)] = value[body_rows:]

        for k in range(whole):
            store(k, difference(k))
        for m in range(split // 2):
            ends = []
            for k in (whole + 2 * m, whole + 2 * m + 1):
                tile[:pairs] = difference(k).astype(own.dtype)
                choice = one_hot(choice_ref[variants_ref[first + k]], flat, own.dtype)
                ends.append(jnp.dot(tile[...], choice, preferred_element_type=jnp.float32)[:pairs])
            store(whole + m, jnp.concatenate(ends, axis=1))
        out[body_rows * slots:] = rest[...].astype(own.dtype)

    smem = pl.BlockSpec(memory_space=pltpu.SMEM)
    vmem = pl.BlockSpec(memory_space=pltpu.VMEM)
    return pl.pallas_call(
        body,
        in_specs=[smem, smem, smem, vmem, vmem, vmem, vmem],
        out_shape=jax.ShapeDtypeStruct((slots * pairs, flat), own.dtype),
        scratch_shapes=[
            pltpu.VMEM(((whole + split) * padded, flat), own.dtype),
            pltpu.VMEM((left * slots, flat), jnp.float32),
            pltpu.VMEM((padded, flat), own.dtype),
        ],
        compiler_params=pltpu.CompilerParams(vmem_limit_bytes=VMEM_BYTES),
        name="antisymmetrize",
    )(place, *schedule(1), own, mirrored, swap_row(flat), choice_rows(flat))


def packed_rows(rows, cols):
    main, over = cols // LANES, cols % LANES
    per = LANES // over
    return main, over, per, -(-rows // per // 16) * 16


def take_tiles(integrals, place, irrep, tile_map, base, whole, split, swapped):
    c_count, virt, cols = integrals.shape
    flat = padded_flat(TILE * TILE)
    half = flat // 2
    blocks = virt // WINDOW
    span = 3 * WINDOW
    whole_target = jnp.asarray(row_targets(whole_pairs(), flat, swapped))
    split_target = jnp.asarray(np.stack([row_targets(split_pairs(v), half, swapped) for v in range(3)]))
    main, over, per, _ = packed_rows(flat, cols)
    sizes = [flat] * whole + [half] * split
    stripes = [max(-(-rows // per), 80) for rows in sizes]

    slots = len(WHOLE) + len(SPLIT)

    def body(place_ref, others_ref, variants_ref, irrep_ref, kept_ref,
             r0, r1, r2, column_ref, whole_ref, split_ref, v0, v1, v2, *refs):
        outs, slab = refs[:-1], refs[-1]
        s = pl.program_id(0)
        row, shard = place_ref[0], place_ref[1]
        entry = row * slots + base + s
        other = others_ref[entry]
        offset = other * TILE % WINDOW
        dropped = jnp.where(kept_ref[row, other] != 0, 0, 1 << 20)
        for q, (r, v) in enumerate(((r0, v0), (r1, v1), (r2, v2))):
            code = jnp.bitwise_xor(r[...], column_ref[...])
            for c in range(c_count):
                wanted = jnp.bitwise_xor(irrep_ref[row * c_count + c], irrep_ref[shard]) + dropped
                kept = jnp.where(code == wanted, v[c].astype(jnp.float32), 0.0)
                slab[span * c + WINDOW * q:span * c + WINDOW * (q + 1), :] = kept.astype(integrals.dtype)

        def pick(target):
            place = lax.broadcasted_iota(jnp.int32, (target.shape[0], span * c_count), 1)
            chosen = jnp.where(place == target + offset, 1.0, 0.0).astype(integrals.dtype)
            return jnp.dot(chosen, slab[...], preferred_element_type=jnp.float32).astype(integrals.dtype)

        def pack(out, rows, stripe, value):
            for b in range(main):
                out[rows * b:rows * (b + 1), :] = value[:, LANES * b:LANES * (b + 1)]
            strips = [value[stripe * i:stripe * (i + 1), LANES * main:] for i in range(rows // stripe)]
            strips += [jnp.zeros_like(strips[0])] * (per - len(strips))
            out[rows * main:, :] = jnp.concatenate(strips, axis=1)

        @pl.when(s < whole)
        def _():
            value = pick(whole_ref[...])
            if swapped:
                for k in range(whole):
                    @pl.when(s == k)
                    def _(k=k):
                        pack(outs[k], flat, stripes[k], value)
            else:
                outs[0][0] = value

        @pl.when(s >= whole)
        def _():
            value = pick(split_ref[variants_ref[entry]])
            for k in range(whole, whole + split):
                @pl.when(s == k)
                def _(k=k):
                    if swapped:
                        pack(outs[k], half, stripes[k], value)
                    else:
                        low = half * ((k - whole) % 2)
                        outs[0][0, low:low + half, :] = value

    def block(q, s, place, others):
        start = others[place[0] * slots + base + s] * TILE
        return jnp.minimum(start // WINDOW + q, blocks - 1)

    def window(q):
        return lambda s, place, others, *_: (0, block(q, s, place, others), 0)

    def code_window(q):
        return lambda s, place, others, *_: (block(q, s, place, others), 0)

    fixed = lambda rank: (lambda s, *_: (0,) * rank)
    if swapped:
        shapes = [(main * rows + stripe, LANES) for rows, stripe in zip(sizes, stripes)]
        out_specs = [pl.BlockSpec(shape, fixed(2)) for shape in shapes]
        out_shape = [jax.ShapeDtypeStruct(shape, integrals.dtype) for shape in shapes]
    else:
        out_specs = [pl.BlockSpec(
            (1, flat, cols), lambda s, *_: (jnp.where(s < whole, s, whole + (s - whole) // 2), 0, 0))]
        out_shape = [jax.ShapeDtypeStruct((whole + split // 2, flat, cols), integrals.dtype)]
    return pl.pallas_call(
        body,
        grid_spec=pltpu.PrefetchScalarGridSpec(
            num_scalar_prefetch=5,
            grid=(whole + split,),
            in_specs=[pl.BlockSpec((WINDOW, 1), code_window(q)) for q in range(3)]
            + [
                pl.BlockSpec((1, cols), fixed(2)),
                pl.BlockSpec((flat, 1), fixed(2)),
                pl.BlockSpec((3, half, 1), fixed(3)),
            ]
            + [pl.BlockSpec((c_count, WINDOW, cols), window(q)) for q in range(3)],
            out_specs=out_specs,
            scratch_shapes=[pltpu.VMEM((span * c_count, cols), integrals.dtype)],
        ),
        out_shape=out_shape,
        compiler_params=pltpu.CompilerParams(vmem_limit_bytes=VMEM_BYTES),
        cost_estimate=pl.CostEstimate(
            flops=2 * (whole + split // 2) * flat * span * c_count * cols,
            bytes_accessed=2 * (whole + split) * span * c_count * cols, transcendentals=0),
        name="take_swapped_tiles" if swapped else "take_own_tiles",
    )(place, *schedule(-1 if swapped else 1), irrep, tile_map, *[irrep[:, None]] * 3, irrep[None, :],
      whole_target, split_target, integrals, integrals, integrals)


def tile_major(t):
    c_count, pairs, virt = t.shape
    tiles = virt // TILE
    flat = -(-c_count * TILE // LANES) * LANES

    def body(t_ref, out_ref):
        for j in range(tiles):
            parts = [t_ref[c, :, TILE * j:TILE * (j + 1)] for c in range(c_count)]
            parts.append(jnp.zeros((pairs, flat - c_count * TILE), t.dtype))
            out_ref[j] = jnp.concatenate(parts, axis=1)

    return pl.pallas_call(
        body,
        out_shape=jax.ShapeDtypeStruct((tiles, pairs, flat), t.dtype),
        compiler_params=pltpu.CompilerParams(vmem_limit_bytes=VMEM_BYTES),
        name="tile_major",
    )(t)


def less(held_ref, out, low, count, other):
    cols = held_ref.shape[2]
    main, over, _, _ = packed_rows(count, cols)
    stripe = other.shape[0] - main * count
    for b in range(main):
        lanes = slice(LANES * b, LANES * (b + 1))
        out[low:low + count, lanes] = (
            held_ref[0, low:low + count, lanes].astype(jnp.float32)
            - other[count * b:count * (b + 1), :].astype(jnp.float32)
        ).astype(out.dtype)
    last = other[count * main:, :].astype(jnp.float32)
    for i in range(count // stripe):
        at = slice(low + stripe * i, low + stripe * (i + 1))
        out[at, LANES * main:] = (
            held_ref[0, at, LANES * main:].astype(jnp.float32) - last[:, over * i:over * (i + 1)]
        ).astype(out.dtype)


def subtract_tiles(held, others):
    slots, flat, cols = held.shape

    def body(held_ref, *refs):
        others_ref, out = refs[:-1], refs[-1]
        for k in range(len(others)):
            @pl.when(pl.program_id(0) == k)
            def _(k=k):
                less(held_ref, out.at[0], 0, flat, others_ref[k])

    tile = pl.BlockSpec((1, flat, cols), lambda k: (k, 0, 0))
    return pl.pallas_call(
        body,
        grid=(len(others),),
        in_specs=[tile] + [pl.BlockSpec(memory_space=pltpu.VMEM) for other in others],
        out_specs=tile,
        out_shape=jax.ShapeDtypeStruct(held.shape, held.dtype),
        input_output_aliases={0: 0},
        compiler_params=pltpu.CompilerParams(vmem_limit_bytes=VMEM_BYTES),
        cost_estimate=pl.CostEstimate(
            flops=len(others) * flat * cols, bytes_accessed=6 * len(others) * flat * cols, transcendentals=0),
        name="subtract_tiles",
    )(held, *others)


def contract(gathered, held, others, ready, body_rows):
    shards, rows, flat = gathered.shape
    slots, _, cols = held.shape
    pairs = rows // slots
    left = pairs - body_rows
    rest_rows = left * slots
    whole = len(WHOLE)
    half = flat // 2
    main, over, per, _ = packed_rows(flat, cols)
    strip = body_rows // per
    tail_rows = padded_tail(body_rows, left, cols)

    def body(main_ref, rest_ref, held_ref, *refs):
        others_ref, (out, weights, left_side, spread, rests, sums, tail) = refs[:-7], refs[-7:]
        slot = pl.program_id(0)

        @pl.when(slot < ready)
        def _():
            weights[...] = held_ref[0]

        for k in range(ready, slots):
            @pl.when(slot == k)
            def _(k=k):
                if k < whole:
                    less(held_ref, weights, 0, flat, others_ref[k - ready])
                else:
                    less(held_ref, weights, 0, half, others_ref[whole - ready + 2 * (k - whole)])
                    less(held_ref, weights, half, half, others_ref[whole - ready + 2 * (k - whole) + 1])

        @pl.when(slot == 0)
        def _():
            sums[...] = jnp.zeros(sums.shape, jnp.float32)
            for b in range(flat // LANES):
                lanes = slice(LANES * b, LANES * (b + 1))
                spread[...] = rest_ref[:, :, lanes].reshape(shards * rest_rows, LANES).astype(jnp.float32)
                for k in range(slots):
                    rests[k, :, lanes] = jnp.concatenate([
                        spread[pl.ds(left * k + i, shards, stride=rest_rows), :] for i in range(left)
                    ], axis=0).astype(rests.dtype)

        left_side[:shards * body_rows] = main_ref[...].reshape(shards * body_rows, flat)
        left_side[shards * body_rows:] = rests[slot]
        sums[...] += jnp.dot(left_side[...], weights[...], preferred_element_type=jnp.float32)

        @pl.when(slot == slots - 1)
        def _():
            total = 0.5 * sums[...]
            full = total[:shards * body_rows].reshape(shards, body_rows, cols)
            folded = jnp.stack([
                total[shards * (body_rows + i):shards * (body_rows + i + 1)] for i in range(left)], axis=1)
            for b in range(main):
                lanes = slice(LANES * b, LANES * (b + 1))
                out[:, body_rows * b:body_rows * (b + 1), :] = full[:, :, lanes].astype(out.dtype)
                tail[:, left * b:left * (b + 1), :] = folded[:, :, lanes]
            at = left * main
            tail[:, at + strip + left:, :] = jnp.zeros((shards, tail_rows - at - strip - left, LANES), jnp.float32)
            for i in range(per):
                tail[:, at:at + strip, over * i:over * (i + 1)] = full[:, strip * i:strip * (i + 1), LANES * main:]
            tail[:, at + strip:at + strip + left, over:] = jnp.zeros((shards, left, LANES - over), jnp.float32)
            tail[:, at + strip:at + strip + left, :over] = folded[:, :, LANES * main:]
            out[:, body_rows * main:, :] = tail[...].astype(out.dtype)

    out_rows = body_rows * main + tail_rows
    return pl.pallas_call(
        body,
        grid=(slots,),
        in_specs=[
            pl.BlockSpec((shards, body_rows, flat), lambda k: (0, k, 0)),
            pl.BlockSpec((shards, rest_rows, flat), lambda k: (0, body_rows * slots // rest_rows, 0)),
            pl.BlockSpec((1, flat, cols), lambda k: (k, 0, 0)),
        ]
        + [pl.BlockSpec(memory_space=pltpu.VMEM) for other in others],
        out_specs=pl.BlockSpec((shards, out_rows, LANES), lambda k: (0, 0, 0)),
        out_shape=jax.ShapeDtypeStruct((shards, out_rows, LANES), gathered.dtype),
        scratch_shapes=[
            pltpu.VMEM((flat, cols), held.dtype),
            pltpu.VMEM((shards * pairs, flat), held.dtype),
            pltpu.VMEM((shards * rest_rows, LANES), jnp.float32),
            pltpu.VMEM((slots, shards * left, flat), held.dtype),
            pltpu.VMEM((shards * pairs, cols), jnp.float32),
            pltpu.VMEM((shards, tail_rows, LANES), jnp.float32),
        ],
        compiler_params=pltpu.CompilerParams(vmem_limit_bytes=VMEM_BYTES),
        cost_estimate=pl.CostEstimate(
            flops=2 * slots * shards * pairs * flat * cols,
            bytes_accessed=2 * gathered.size + 2 * held.size, transcendentals=0),
        name="contract",
    )(gathered, gathered, held, *others)


def padded_tail(body_rows, left, cols):
    main, over, per, _ = packed_rows(body_rows, cols)
    return -(-(left * main + body_rows // per + left) // 16) * 16


def add_pieces(pieces, body_rows, left, cols):
    main, over, per, _ = packed_rows(body_rows, cols)
    strip = body_rows // per

    def body(pieces_ref, out, scratch):
        total = jnp.sum(pieces_ref[...].astype(jnp.float32), axis=0)
        tail = total[body_rows * main:]
        at = left * main
        for b in range(main):
            lanes = slice(LANES * b, LANES * (b + 1))
            scratch[:body_rows, lanes] = total[body_rows * b:body_rows * (b + 1)]
            scratch[body_rows:, lanes] = tail[left * b:left * (b + 1)]
        for i in range(per):
            scratch[strip * i:strip * (i + 1), LANES * main:] = tail[at:at + strip, over * i:over * (i + 1)]
        scratch[body_rows:, LANES * main:] = tail[at + strip:at + strip + left, :over]
        out[...] = scratch[...].astype(out.dtype)

    return pl.pallas_call(
        body,
        out_shape=jax.ShapeDtypeStruct((body_rows + left, cols), pieces.dtype),
        scratch_shapes=[pltpu.VMEM((body_rows + left, cols), jnp.float32)],
        compiler_params=pltpu.CompilerParams(vmem_limit_bytes=VMEM_BYTES),
        name="add_pieces",
    )(pieces)


BODY_ROWS = 48
EARLY = 5


def local(t_amps, integrals, virt_irrep, tile_map):
    own_rows, c_count, virt_count = t_amps.shape
    own_cols = integrals.shape[2]
    assert c_count == TILE and own_cols == virt_count
    whole, split = len(WHOLE), len(SPLIT)
    place = jnp.stack([lax.axis_index("row"), lax.axis_index(("col", "depth"))]).astype(jnp.int32)

    own = tile_major(jnp.transpose(t_amps, (1, 0, 2)))
    mirrored = lax.all_to_all(own, "row", split_axis=0, concat_axis=0, tiled=True)
    sent_whole = take_tiles(integrals, place, virt_irrep, tile_map, 0, whole, 0, True)
    mirrored, sent_whole = lax.optimization_barrier((mirrored, sent_whole))
    part = antisymmetrize(own, mirrored, place, BODY_ROWS)
    part, sent_whole, place = lax.optimization_barrier((part, sent_whole, place))
    gathered = lax.all_gather(part, ("col", "depth"), axis=0, tiled=False)

    def exchange(offsets, tiles):
        moved = []
        for offset, tile in zip(offsets, tiles):
            if offset != (0, 0):
                moves = [(neighbour(r, offset, 1), r) for r in range(SIDE * SIDE)]
                tile = lax.ppermute(tile, "row", moves)
            moved.append(tile)
        return moved

    others = exchange(WHOLE[:EARLY], sent_whole[:EARLY])
    sent_split = take_tiles(integrals, place, virt_irrep, tile_map, whole, 0, split, True)
    others[0], sent_split, last, place = lax.optimization_barrier(
        (others[0], sent_split, sent_whole[EARLY:], place))
    late = exchange(WHOLE[EARLY:], last)
    held = take_tiles(integrals, place, virt_irrep, tile_map, 0, whole, split, False)[0]
    held, sent_split = lax.optimization_barrier((held, sent_split))
    late += exchange(SPLIT, sent_split)
    held = subtract_tiles(held, others)
    result = contract(gathered, held, late, EARLY, BODY_ROWS)
    pieces = lax.all_to_all(result, "row", split_axis=0, concat_axis=0, tiled=True)
    return add_pieces(pieces, BODY_ROWS, own_rows - BODY_ROWS, own_cols)


def solution(mesh):
    placed = (P(("col", "depth"), "row", None), P("row", None, ("col", "depth")), P(), P())
    return jax.shard_map(
        local, mesh=mesh, in_specs=placed, out_specs=P("row", ("col", "depth")), check_vma=False
    )
```

```python
import jax
import jax.numpy as jnp
import numpy as np
from jax import lax
from jax.experimental import pallas as pl
from jax.experimental.pallas import tpu as pltpu
from jax.sharding import PartitionSpec as P

TILE = 25
LANES = 128
WINDOW = 16
SIDE = 4
WHOLE = ((0, 1), (1, 0), (3, 3), (1, 3), (3, 2), (2, 1))
SPLIT = ((0, 2), (2, 0), (2, 2), (0, 0))
NOWHERE = -(1 << 20)
VMEM_BYTES = 52 * 1024 * 1024


def split_pairs(variant):
    chosen = [(u, v) for u in range(TILE) for v in range(u + 1, TILE)]
    middle = (TILE + 1) // 2
    if variant == 0:
        chosen += [(u, u) for u in range(middle)]
    elif variant == 1:
        chosen += [(u, u) for u in range(middle, TILE)]
    return chosen


def whole_pairs():
    return [(u, v) for u in range(TILE) for v in range(TILE)]


def padded_flat(count):
    return -(-count // LANES) * LANES


def row_targets(pairs, rows, swapped):
    target = np.full((rows, 1), NOWHERE, np.int32)
    for k, (u, v) in enumerate(pairs):
        target[k, 0] = v * 3 * WINDOW + u if swapped else u * 3 * WINDOW + v
    return target


def swap_row(flat):
    row = np.full((1, flat), NOWHERE, np.int32)
    for u, v in whole_pairs():
        row[0, v * TILE + u] = u * TILE + v
    return jnp.asarray(row)


def choice_rows(flat):
    rows = np.full((3, 1, flat // 2), NOWHERE, np.int32)
    for variant in range(3):
        for k, (u, v) in enumerate(split_pairs(variant)):
            rows[variant, 0, k] = u * TILE + v
    return jnp.asarray(rows)


def one_hot(row, count, dtype):
    places = lax.broadcasted_iota(jnp.int32, (count, row.shape[1]), 0)
    return jnp.where(places == row, 1.0, 0.0).astype(dtype)


def neighbour(row, offset, sign):
    y = (row // SIDE + sign * offset[0]) % SIDE
    x = (row % SIDE + sign * offset[1]) % SIDE
    return y * SIDE + x


def schedule(sign):
    others = np.zeros((SIDE * SIDE, len(WHOLE) + len(SPLIT)), np.int32)
    variants = np.zeros_like(others)
    for row in range(SIDE * SIDE):
        for k, offset in enumerate(WHOLE + SPLIT):
            other = neighbour(row, offset, sign)
            worker, source = (row, other) if sign == 1 else (other, row)
            others[row, k] = other
            variants[row, k] = 2 if offset == (0, 0) else int(worker > source)
    return jnp.asarray(others.ravel()), jnp.asarray(variants.ravel())


def antisymmetrize(own, mirrored, place, body_rows):
    tiles, pairs, flat = own.shape
    whole, split = len(WHOLE), len(SPLIT)
    slots = whole + split // 2
    left = pairs - body_rows
    padded = -(-pairs // 16) * 16

    def body(place_ref, places_ref, variants_ref, own_ref, mirrored_ref, swap_ref, choice_ref, out, stack, rest, tile):
        first = place_ref[0] * (whole + split)
        for k in range(whole + split):
            stack[padded * k:padded * k + pairs] = mirrored_ref[places_ref[first + k]]
        swap = one_hot(swap_ref[...], flat, own.dtype)
        swapped = jnp.dot(stack[...], swap, preferred_element_type=jnp.float32)

        def difference(k):
            return own_ref[places_ref[first + k]].astype(jnp.float32) - swapped[padded * k:padded * k + pairs]

        def store(slot, value):
            out[body_rows * slot:body_rows * (slot + 1)] = value[:body_rows].astype(own.dtype)
            rest[left * slot:left * (slot + 1)] = value[body_rows:]

        for k in range(whole):
            store(k, difference(k))
        for m in range(split // 2):
            ends = []
            for k in (whole + 2 * m, whole + 2 * m + 1):
                tile[:pairs] = difference(k).astype(own.dtype)
                choice = one_hot(choice_ref[variants_ref[first + k]], flat, own.dtype)
                ends.append(jnp.dot(tile[...], choice, preferred_element_type=jnp.float32)[:pairs])
            store(whole + m, jnp.concatenate(ends, axis=1))
        out[body_rows * slots:] = rest[...].astype(own.dtype)

    smem = pl.BlockSpec(memory_space=pltpu.SMEM)
    vmem = pl.BlockSpec(memory_space=pltpu.VMEM)
    return pl.pallas_call(
        body,
        in_specs=[smem, smem, smem, vmem, vmem, vmem, vmem],
        out_shape=jax.ShapeDtypeStruct((slots * pairs, flat), own.dtype),
        scratch_shapes=[
            pltpu.VMEM(((whole + split) * padded, flat), own.dtype),
            pltpu.VMEM((left * slots, flat), jnp.float32),
            pltpu.VMEM((padded, flat), own.dtype),
        ],
        compiler_params=pltpu.CompilerParams(vmem_limit_bytes=VMEM_BYTES),
        name="antisymmetrize",
    )(place, *schedule(1), own, mirrored, swap_row(flat), choice_rows(flat))


def packed_rows(rows, cols):
    main, over = cols // LANES, cols % LANES
    per = LANES // over
    return main, over, per, -(-rows // per // 16) * 16


def take_tiles(integrals, place, irrep, tile_map, base, whole, split, swapped):
    c_count, virt, cols = integrals.shape
    flat = padded_flat(TILE * TILE)
    half = flat // 2
    blocks = virt // WINDOW
    span = 3 * WINDOW
    whole_target = jnp.asarray(row_targets(whole_pairs(), flat, swapped))
    split_target = jnp.asarray(np.stack([row_targets(split_pairs(v), half, swapped) for v in range(3)]))
    main, over, per, _ = packed_rows(flat, cols)
    sizes = [flat] * whole + [half] * split
    stripes = [max(-(-rows // per), 80) for rows in sizes]

    slots = len(WHOLE) + len(SPLIT)

    def body(place_ref, others_ref, variants_ref, irrep_ref, kept_ref,
             r0, r1, r2, column_ref, whole_ref, split_ref, v0, v1, v2, *refs):
        outs, slab = refs[:-1], refs[-1]
        s = pl.program_id(0)
        row, shard = place_ref[0], place_ref[1]
        entry = row * slots + base + s
        other = others_ref[entry]
        offset = other * TILE % WINDOW
        dropped = jnp.where(kept_ref[row, other] != 0, 0, 1 << 20)
        for q, (r, v) in enumerate(((r0, v0), (r1, v1), (r2, v2))):
            code = jnp.bitwise_xor(r[...], column_ref[...])
            for c in range(c_count):
                wanted = jnp.bitwise_xor(irrep_ref[row * c_count + c], irrep_ref[shard]) + dropped
                kept = jnp.where(code == wanted, v[c].astype(jnp.float32), 0.0)
                slab[span * c + WINDOW * q:span * c + WINDOW * (q + 1), :] = kept.astype(integrals.dtype)

        def pick(target):
            place = lax.broadcasted_iota(jnp.int32, (target.shape[0], span * c_count), 1)
            chosen = jnp.where(place == target + offset, 1.0, 0.0).astype(integrals.dtype)
            return jnp.dot(chosen, slab[...], preferred_element_type=jnp.float32).astype(integrals.dtype)

        def pack(out, rows, stripe, value):
            for b in range(main):
                out[rows * b:rows * (b + 1), :] = value[:, LANES * b:LANES * (b + 1)]
            strips = [value[stripe * i:stripe * (i + 1), LANES * main:] for i in range(rows // stripe)]
            strips += [jnp.zeros_like(strips[0])] * (per - len(strips))
            out[rows * main:, :] = jnp.concatenate(strips, axis=1)

        @pl.when(s < whole)
        def _():
            value = pick(whole_ref[...])
            if swapped:
                for k in range(whole):
                    @pl.when(s == k)
                    def _(k=k):
                        pack(outs[k], flat, stripes[k], value)
            else:
                outs[0][0] = value

        @pl.when(s >= whole)
        def _():
            value = pick(split_ref[variants_ref[entry]])
            for k in range(whole, whole + split):
                @pl.when(s == k)
                def _(k=k):
                    if swapped:
                        pack(outs[k], half, stripes[k], value)
                    else:
                        low = half * ((k - whole) % 2)
                        outs[0][0, low:low + half, :] = value

    def block(q, s, place, others):
        start = others[place[0] * slots + base + s] * TILE
        return jnp.minimum(start // WINDOW + q, blocks - 1)

    def window(q):
        return lambda s, place, others, *_: (0, block(q, s, place, others), 0)

    def code_window(q):
        return lambda s, place, others, *_: (block(q, s, place, others), 0)

    fixed = lambda rank: (lambda s, *_: (0,) * rank)
    if swapped:
        shapes = [(main * rows + stripe, LANES) for rows, stripe in zip(sizes, stripes)]
        out_specs = [pl.BlockSpec(shape, fixed(2)) for shape in shapes]
        out_shape = [jax.ShapeDtypeStruct(shape, integrals.dtype) for shape in shapes]
    else:
        out_specs = [pl.BlockSpec(
            (1, flat, cols), lambda s, *_: (jnp.where(s < whole, s, whole + (s - whole) // 2), 0, 0))]
        out_shape = [jax.ShapeDtypeStruct((whole + split // 2, flat, cols), integrals.dtype)]
    return pl.pallas_call(
        body,
        grid_spec=pltpu.PrefetchScalarGridSpec(
            num_scalar_prefetch=5,
            grid=(whole + split,),
            in_specs=[pl.BlockSpec((WINDOW, 1), code_window(q)) for q in range(3)]
            + [
                pl.BlockSpec((1, cols), fixed(2)),
                pl.BlockSpec((flat, 1), fixed(2)),
                pl.BlockSpec((3, half, 1), fixed(3)),
            ]
            + [pl.BlockSpec((c_count, WINDOW, cols), window(q)) for q in range(3)],
            out_specs=out_specs,
            scratch_shapes=[pltpu.VMEM((span * c_count, cols), integrals.dtype)],
        ),
        out_shape=out_shape,
        compiler_params=pltpu.CompilerParams(vmem_limit_bytes=VMEM_BYTES),
        cost_estimate=pl.CostEstimate(
            flops=2 * (whole + split // 2) * flat * span * c_count * cols,
            bytes_accessed=2 * (whole + split) * span * c_count * cols, transcendentals=0),
        name="take_swapped_tiles" if swapped else "take_own_tiles",
    )(place, *schedule(-1 if swapped else 1), irrep, tile_map, *[irrep[:, None]] * 3, irrep[None, :],
      whole_target, split_target, integrals, integrals, integrals)


def tile_major(t):
    c_count, pairs, virt = t.shape
    tiles = virt // TILE
    flat = -(-c_count * TILE // LANES) * LANES

    def body(t_ref, out_ref):
        for j in range(tiles):
            parts = [t_ref[c, :, TILE * j:TILE * (j + 1)] for c in range(c_count)]
            parts.append(jnp.zeros((pairs, flat - c_count * TILE), t.dtype))
            out_ref[j] = jnp.concatenate(parts, axis=1)

    return pl.pallas_call(
        body,
        out_shape=jax.ShapeDtypeStruct((tiles, pairs, flat), t.dtype),
        compiler_params=pltpu.CompilerParams(vmem_limit_bytes=VMEM_BYTES),
        name="tile_major",
    )(t)


def contract(gathered, held, others, body_rows):
    shards, rows, flat = gathered.shape
    slots, _, cols = held.shape
    pairs = rows // slots
    left = pairs - body_rows
    rest_rows = left * slots
    whole = len(WHOLE)
    half = flat // 2
    main, over, per, _ = packed_rows(flat, cols)
    strip = body_rows // per
    tail_rows = padded_tail(body_rows, left, cols)

    def body(main_ref, rest_ref, held_ref, *refs):
        others_ref, (out, weights, left_side, spread, rests, sums, tail) = refs[:-7], refs[-7:]
        slot = pl.program_id(0)

        def less(low, count, other):
            stripe = other.shape[0] - main * count
            for b in range(main):
                lanes = slice(LANES * b, LANES * (b + 1))
                weights[low:low + count, lanes] = (
                    held_ref[0, low:low + count, lanes].astype(jnp.float32)
                    - other[count * b:count * (b + 1), :].astype(jnp.float32)
                ).astype(held.dtype)
            last = other[count * main:, :].astype(jnp.float32)
            for i in range(count // stripe):
                at = slice(low + stripe * i, low + stripe * (i + 1))
                weights[at, LANES * main:] = (
                    held_ref[0, at, LANES * main:].astype(jnp.float32) - last[:, over * i:over * (i + 1)]
                ).astype(held.dtype)

        for k in range(slots):
            @pl.when(slot == k)
            def _(k=k):
                if k < whole:
                    less(0, flat, others_ref[k])
                else:
                    less(0, half, others_ref[whole + 2 * (k - whole)])
                    less(half, half, others_ref[whole + 2 * (k - whole) + 1])

        @pl.when(slot == 0)
        def _():
            sums[...] = jnp.zeros(sums.shape, jnp.float32)
            for b in range(flat // LANES):
                lanes = slice(LANES * b, LANES * (b + 1))
                spread[...] = rest_ref[:, :, lanes].reshape(shards * rest_rows, LANES).astype(jnp.float32)
                for k in range(slots):
                    rests[k, :, lanes] = jnp.concatenate([
                        spread[pl.ds(left * k + i, shards, stride=rest_rows), :] for i in range(left)
                    ], axis=0).astype(rests.dtype)

        left_side[:shards * body_rows] = main_ref[...].reshape(shards * body_rows, flat)
        left_side[shards * body_rows:] = rests[slot]
        sums[...] += jnp.dot(left_side[...], weights[...], preferred_element_type=jnp.float32)

        @pl.when(slot == slots - 1)
        def _():
            total = 0.5 * sums[...]
            full = total[:shards * body_rows].reshape(shards, body_rows, cols)
            folded = jnp.stack([
                total[shards * (body_rows + i):shards * (body_rows + i + 1)] for i in range(left)], axis=1)
            for b in range(main):
                lanes = slice(LANES * b, LANES * (b + 1))
                out[:, body_rows * b:body_rows * (b + 1), :] = full[:, :, lanes].astype(out.dtype)
                tail[:, left * b:left * (b + 1), :] = folded[:, :, lanes]
            at = left * main
            tail[:, at + strip + left:, :] = jnp.zeros((shards, tail_rows - at - strip - left, LANES), jnp.float32)
            for i in range(per):
                tail[:, at:at + strip, over * i:over * (i + 1)] = full[:, strip * i:strip * (i + 1), LANES * main:]
            tail[:, at + strip:at + strip + left, over:] = jnp.zeros((shards, left, LANES - over), jnp.float32)
            tail[:, at + strip:at + strip + left, :over] = folded[:, :, LANES * main:]
            out[:, body_rows * main:, :] = tail[...].astype(out.dtype)

    out_rows = body_rows * main + tail_rows
    return pl.pallas_call(
        body,
        grid=(slots,),
        in_specs=[
            pl.BlockSpec((shards, body_rows, flat), lambda k: (0, k, 0)),
            pl.BlockSpec((shards, rest_rows, flat), lambda k: (0, body_rows * slots // rest_rows, 0)),
            pl.BlockSpec((1, flat, cols), lambda k: (k, 0, 0)),
        ]
        + [pl.BlockSpec(memory_space=pltpu.VMEM) for other in others],
        out_specs=pl.BlockSpec((shards, out_rows, LANES), lambda k: (0, 0, 0)),
        out_shape=jax.ShapeDtypeStruct((shards, out_rows, LANES), gathered.dtype),
        scratch_shapes=[
            pltpu.VMEM((flat, cols), held.dtype),
            pltpu.VMEM((shards * pairs, flat), held.dtype),
            pltpu.VMEM((shards * rest_rows, LANES), jnp.float32),
            pltpu.VMEM((slots, shards * left, flat), held.dtype),
            pltpu.VMEM((shards * pairs, cols), jnp.float32),
            pltpu.VMEM((shards, tail_rows, LANES), jnp.float32),
        ],
        compiler_params=pltpu.CompilerParams(vmem_limit_bytes=VMEM_BYTES),
        cost_estimate=pl.CostEstimate(
            flops=2 * slots * shards * pairs * flat * cols,
            bytes_accessed=2 * gathered.size + 2 * held.size, transcendentals=0),
        name="contract",
    )(gathered, gathered, held, *others)


def padded_tail(body_rows, left, cols):
    main, over, per, _ = packed_rows(body_rows, cols)
    return -(-(left * main + body_rows // per + left) // 16) * 16


def add_pieces(pieces, body_rows, left, cols):
    main, over, per, _ = packed_rows(body_rows, cols)
    strip = body_rows // per

    def body(pieces_ref, out, scratch):
        total = jnp.sum(pieces_ref[...].astype(jnp.float32), axis=0)
        tail = total[body_rows * main:]
        at = left * main
        for b in range(main):
            lanes = slice(LANES * b, LANES * (b + 1))
            scratch[:body_rows, lanes] = total[body_rows * b:body_rows * (b + 1)]
            scratch[body_rows:, lanes] = tail[left * b:left * (b + 1)]
        for i in range(per):
            scratch[strip * i:strip * (i + 1), LANES * main:] = tail[at:at + strip, over * i:over * (i + 1)]
        scratch[body_rows:, LANES * main:] = tail[at + strip:at + strip + left, :over]
        out[...] = scratch[...].astype(out.dtype)

    return pl.pallas_call(
        body,
        out_shape=jax.ShapeDtypeStruct((body_rows + left, cols), pieces.dtype),
        scratch_shapes=[pltpu.VMEM((body_rows + left, cols), jnp.float32)],
        compiler_params=pltpu.CompilerParams(vmem_limit_bytes=VMEM_BYTES),
        name="add_pieces",
    )(pieces)


BODY_ROWS = 48
EARLY = 1


def local(t_amps, integrals, virt_irrep, tile_map):
    own_rows, c_count, virt_count = t_amps.shape
    own_cols = integrals.shape[2]
    assert c_count == TILE and own_cols == virt_count
    whole, split = len(WHOLE), len(SPLIT)
    place = jnp.stack([lax.axis_index("row"), lax.axis_index(("col", "depth"))]).astype(jnp.int32)

    own = tile_major(jnp.transpose(t_amps, (1, 0, 2)))
    mirrored = lax.all_to_all(own, "row", split_axis=0, concat_axis=0, tiled=True)
    sent_whole = take_tiles(integrals, place, virt_irrep, tile_map, 0, whole, 0, True)
    mirrored, sent_whole = lax.optimization_barrier((mirrored, sent_whole))
    part = antisymmetrize(own, mirrored, place, BODY_ROWS)
    part, sent_whole, place = lax.optimization_barrier((part, sent_whole, place))
    gathered = lax.all_gather(part, ("col", "depth"), axis=0, tiled=False)

    def exchange(offsets, tiles):
        moved = []
        for offset, tile in zip(offsets, tiles):
            if offset != (0, 0):
                moves = [(neighbour(r, offset, 1), r) for r in range(SIDE * SIDE)]
                tile = lax.ppermute(tile, "row", moves)
            moved.append(tile)
        return moved

    others = exchange(WHOLE, sent_whole)
    held = take_tiles(integrals, place, virt_irrep, tile_map, 0, whole, split, False)[0]
    held, place = lax.optimization_barrier((held, place))
    sent_split = take_tiles(integrals, place, virt_irrep, tile_map, whole, 0, split, True)
    others[:EARLY], sent_split = lax.optimization_barrier((others[:EARLY], sent_split))
    others = others + exchange(SPLIT, sent_split)
    result = contract(gathered, held, others, BODY_ROWS)
    pieces = lax.all_to_all(result, "row", split_axis=0, concat_axis=0, tiled=True)
    return add_pieces(pieces, BODY_ROWS, own_rows - BODY_ROWS, own_cols)


def solution(mesh):
    placed = (P(("col", "depth"), "row", None), P("row", None, ("col", "depth")), P(), P())
    return jax.shard_map(
        local, mesh=mesh, in_specs=placed, out_specs=P("row", ("col", "depth")), check_vma=False
    )
```

```python
import jax
import jax.numpy as jnp
import numpy as np
from jax import lax
from jax.experimental import pallas as pl
from jax.experimental.pallas import tpu as pltpu
from jax.sharding import PartitionSpec as P

TILE = 25
LANES = 128
WINDOW = 16
SIDE = 4
WHOLE = ((0, 1), (3, 2), (2, 1), (3, 3), (1, 3), (1, 0))
SPLIT = ((0, 2), (2, 0), (2, 2), (0, 0))
NOWHERE = -(1 << 20)
VMEM_BYTES = 52 * 1024 * 1024


def split_pairs(variant):
    chosen = [(u, v) for u in range(TILE) for v in range(u + 1, TILE)]
    middle = (TILE + 1) // 2
    if variant == 0:
        chosen += [(u, u) for u in range(middle)]
    elif variant == 1:
        chosen += [(u, u) for u in range(middle, TILE)]
    return chosen


def whole_pairs():
    return [(u, v) for u in range(TILE) for v in range(TILE)]


def padded_flat(count):
    return -(-count // LANES) * LANES


def row_targets(pairs, rows, swapped):
    target = np.full((rows, 1), NOWHERE, np.int32)
    for k, (u, v) in enumerate(pairs):
        target[k, 0] = v * 3 * WINDOW + u if swapped else u * 3 * WINDOW + v
    return target


def swap_row(flat):
    row = np.full((1, flat), NOWHERE, np.int32)
    for u, v in whole_pairs():
        row[0, v * TILE + u] = u * TILE + v
    return jnp.asarray(row)


def choice_rows(flat):
    rows = np.full((3, 1, flat // 2), NOWHERE, np.int32)
    for variant in range(3):
        for k, (u, v) in enumerate(split_pairs(variant)):
            rows[variant, 0, k] = u * TILE + v
    return jnp.asarray(rows)


def one_hot(row, count, dtype):
    places = lax.broadcasted_iota(jnp.int32, (count, row.shape[1]), 0)
    return jnp.where(places == row, 1.0, 0.0).astype(dtype)


def neighbour(row, offset, sign):
    y = (row // SIDE + sign * offset[0]) % SIDE
    x = (row % SIDE + sign * offset[1]) % SIDE
    return y * SIDE + x


def schedule(sign):
    others = np.zeros((SIDE * SIDE, len(WHOLE) + len(SPLIT)), np.int32)
    variants = np.zeros_like(others)
    for row in range(SIDE * SIDE):
        for k, offset in enumerate(WHOLE + SPLIT):
            other = neighbour(row, offset, sign)
            worker, source = (row, other) if sign == 1 else (other, row)
            others[row, k] = other
            variants[row, k] = 2 if offset == (0, 0) else int(worker > source)
    return jnp.asarray(others.ravel()), jnp.asarray(variants.ravel())


def antisymmetrize(own, mirrored, place, body_rows):
    tiles, pairs, flat = own.shape
    whole, split = len(WHOLE), len(SPLIT)
    slots = whole + split // 2
    left = pairs - body_rows
    padded = -(-pairs // 16) * 16

    def body(place_ref, places_ref, variants_ref, own_ref, mirrored_ref, swap_ref, choice_ref, out, stack, rest, tile):
        first = place_ref[0] * (whole + split)
        for k in range(whole + split):
            stack[padded * k:padded * k + pairs] = mirrored_ref[places_ref[first + k]]
        swap = one_hot(swap_ref[...], flat, own.dtype)
        swapped = jnp.dot(stack[...], swap, preferred_element_type=jnp.float32)

        def difference(k):
            return own_ref[places_ref[first + k]].astype(jnp.float32) - swapped[padded * k:padded * k + pairs]

        def store(slot, value):
            out[body_rows * slot:body_rows * (slot + 1)] = value[:body_rows].astype(own.dtype)
            rest[left * slot:left * (slot + 1)] = value[body_rows:]

        for k in range(whole):
            store(k, difference(k))
        for m in range(split // 2):
            ends = []
            for k in (whole + 2 * m, whole + 2 * m + 1):
                tile[:pairs] = difference(k).astype(own.dtype)
                choice = one_hot(choice_ref[variants_ref[first + k]], flat, own.dtype)
                ends.append(jnp.dot(tile[...], choice, preferred_element_type=jnp.float32)[:pairs])
            store(whole + m, jnp.concatenate(ends, axis=1))
        out[body_rows * slots:] = rest[...].astype(own.dtype)

    smem = pl.BlockSpec(memory_space=pltpu.SMEM)
    vmem = pl.BlockSpec(memory_space=pltpu.VMEM)
    return pl.pallas_call(
        body,
        in_specs=[smem, smem, smem, vmem, vmem, vmem, vmem],
        out_shape=jax.ShapeDtypeStruct((slots * pairs, flat), own.dtype),
        scratch_shapes=[
            pltpu.VMEM(((whole + split) * padded, flat), own.dtype),
            pltpu.VMEM((left * slots, flat), jnp.float32),
            pltpu.VMEM((padded, flat), own.dtype),
        ],
        compiler_params=pltpu.CompilerParams(vmem_limit_bytes=VMEM_BYTES),
        name="antisymmetrize",
    )(place, *schedule(1), own, mirrored, swap_row(flat), choice_rows(flat))


def packed_rows(rows, cols):
    main, over = cols // LANES, cols % LANES
    per = LANES // over
    return main, over, per, -(-rows // per // 16) * 16


def take_tiles(integrals, place, irrep, tile_map, base, whole, split, swapped):
    c_count, virt, cols = integrals.shape
    flat = padded_flat(TILE * TILE)
    half = flat // 2
    blocks = virt // WINDOW
    span = 3 * WINDOW
    whole_target = jnp.asarray(row_targets(whole_pairs(), flat, swapped))
    split_target = jnp.asarray(np.stack([row_targets(split_pairs(v), half, swapped) for v in range(3)]))
    main, over, per, _ = packed_rows(flat, cols)
    sizes = [flat] * whole + [half] * split
    stripes = [max(-(-rows // per), 80) for rows in sizes]

    slots = len(WHOLE) + len(SPLIT)

    def body(place_ref, others_ref, variants_ref, irrep_ref, kept_ref,
             r0, r1, r2, column_ref, whole_ref, split_ref, v0, v1, v2, *refs):
        outs, slab = refs[:-1], refs[-1]
        s = pl.program_id(0)
        row, shard = place_ref[0], place_ref[1]
        entry = row * slots + base + s
        other = others_ref[entry]
        offset = other * TILE % WINDOW
        dropped = jnp.where(kept_ref[row, other] != 0, 0, 1 << 20)
        for q, (r, v) in enumerate(((r0, v0), (r1, v1), (r2, v2))):
            code = jnp.bitwise_xor(r[...], column_ref[...])
            for c in range(c_count):
                wanted = jnp.bitwise_xor(irrep_ref[row * c_count + c], irrep_ref[shard]) + dropped
                kept = jnp.where(code == wanted, v[c].astype(jnp.float32), 0.0)
                slab[span * c + WINDOW * q:span * c + WINDOW * (q + 1), :] = kept.astype(integrals.dtype)

        def pick(target):
            place = lax.broadcasted_iota(jnp.int32, (target.shape[0], span * c_count), 1)
            chosen = jnp.where(place == target + offset, 1.0, 0.0).astype(integrals.dtype)
            return jnp.dot(chosen, slab[...], preferred_element_type=jnp.float32).astype(integrals.dtype)

        def pack(out, rows, stripe, value):
            for b in range(main):
                out[rows * b:rows * (b + 1), :] = value[:, LANES * b:LANES * (b + 1)]
            strips = [value[stripe * i:stripe * (i + 1), LANES * main:] for i in range(rows // stripe)]
            strips += [jnp.zeros_like(strips[0])] * (per - len(strips))
            out[rows * main:, :] = jnp.concatenate(strips, axis=1)

        @pl.when(s < whole)
        def _():
            value = pick(whole_ref[...])
            if swapped:
                for k in range(whole):
                    @pl.when(s == k)
                    def _(k=k):
                        pack(outs[k], flat, stripes[k], value)
            else:
                outs[0][0] = value

        @pl.when(s >= whole)
        def _():
            value = pick(split_ref[variants_ref[entry]])
            for k in range(whole, whole + split):
                @pl.when(s == k)
                def _(k=k):
                    if swapped:
                        pack(outs[k], half, stripes[k], value)
                    else:
                        low = half * ((k - whole) % 2)
                        outs[0][0, low:low + half, :] = value

    def block(q, s, place, others):
        start = others[place[0] * slots + base + s] * TILE
        return jnp.minimum(start // WINDOW + q, blocks - 1)

    def window(q):
        return lambda s, place, others, *_: (0, block(q, s, place, others), 0)

    def code_window(q):
        return lambda s, place, others, *_: (block(q, s, place, others), 0)

    fixed = lambda rank: (lambda s, *_: (0,) * rank)
    if swapped:
        shapes = [(main * rows + stripe, LANES) for rows, stripe in zip(sizes, stripes)]
        out_specs = [pl.BlockSpec(shape, fixed(2)) for shape in shapes]
        out_shape = [jax.ShapeDtypeStruct(shape, integrals.dtype) for shape in shapes]
    else:
        out_specs = [pl.BlockSpec(
            (1, flat, cols), lambda s, *_: (jnp.where(s < whole, s, whole + (s - whole) // 2), 0, 0))]
        out_shape = [jax.ShapeDtypeStruct((whole + split // 2, flat, cols), integrals.dtype)]
    return pl.pallas_call(
        body,
        grid_spec=pltpu.PrefetchScalarGridSpec(
            num_scalar_prefetch=5,
            grid=(whole + split,),
            in_specs=[pl.BlockSpec((WINDOW, 1), code_window(q)) for q in range(3)]
            + [
                pl.BlockSpec((1, cols), fixed(2)),
                pl.BlockSpec((flat, 1), fixed(2)),
                pl.BlockSpec((3, half, 1), fixed(3)),
            ]
            + [pl.BlockSpec((c_count, WINDOW, cols), window(q)) for q in range(3)],
            out_specs=out_specs,
            scratch_shapes=[pltpu.VMEM((span * c_count, cols), integrals.dtype)],
        ),
        out_shape=out_shape,
        compiler_params=pltpu.CompilerParams(vmem_limit_bytes=VMEM_BYTES),
        cost_estimate=pl.CostEstimate(
            flops=2 * (whole + split // 2) * flat * span * c_count * cols,
            bytes_accessed=2 * (whole + split) * span * c_count * cols, transcendentals=0),
        name="take_swapped_tiles" if swapped else "take_own_tiles",
    )(place, *schedule(-1 if swapped else 1), irrep, tile_map, *[irrep[:, None]] * 3, irrep[None, :],
      whole_target, split_target, integrals, integrals, integrals)


def tile_major(t):
    c_count, pairs, virt = t.shape
    tiles = virt // TILE
    flat = -(-c_count * TILE // LANES) * LANES

    def body(t_ref, out_ref):
        for j in range(tiles):
            parts = [t_ref[c, :, TILE * j:TILE * (j + 1)] for c in range(c_count)]
            parts.append(jnp.zeros((pairs, flat - c_count * TILE), t.dtype))
            out_ref[j] = jnp.concatenate(parts, axis=1)

    return pl.pallas_call(
        body,
        out_shape=jax.ShapeDtypeStruct((tiles, pairs, flat), t.dtype),
        compiler_params=pltpu.CompilerParams(vmem_limit_bytes=VMEM_BYTES),
        name="tile_major",
    )(t)


def contract(gathered, held, others, body_rows):
    shards, rows, flat = gathered.shape
    slots, _, cols = held.shape
    pairs = rows // slots
    left = pairs - body_rows
    rest_rows = left * slots
    whole = len(WHOLE)
    half = flat // 2
    main, over, per, _ = packed_rows(flat, cols)
    strip = body_rows // per
    tail_rows = padded_tail(body_rows, left, cols)

    def body(main_ref, rest_ref, held_ref, *refs):
        others_ref, (out, weights, left_side, spread, rests, sums, tail) = refs[:-7], refs[-7:]
        slot = pl.program_id(0)

        def less(low, count, other):
            stripe = other.shape[0] - main * count
            for b in range(main):
                lanes = slice(LANES * b, LANES * (b + 1))
                weights[low:low + count, lanes] = (
                    held_ref[0, low:low + count, lanes].astype(jnp.float32)
                    - other[count * b:count * (b + 1), :].astype(jnp.float32)
                ).astype(held.dtype)
            last = other[count * main:, :].astype(jnp.float32)
            for i in range(count // stripe):
                at = slice(low + stripe * i, low + stripe * (i + 1))
                weights[at, LANES * main:] = (
                    held_ref[0, at, LANES * main:].astype(jnp.float32) - last[:, over * i:over * (i + 1)]
                ).astype(held.dtype)

        for k in range(slots):
            @pl.when(slot == k)
            def _(k=k):
                if k < whole:
                    less(0, flat, others_ref[k])
                else:
                    less(0, half, others_ref[whole + 2 * (k - whole)])
                    less(half, half, others_ref[whole + 2 * (k - whole) + 1])

        @pl.when(slot == 0)
        def _():
            sums[...] = jnp.zeros(sums.shape, jnp.float32)
            for b in range(flat // LANES):
                lanes = slice(LANES * b, LANES * (b + 1))
                spread[...] = rest_ref[:, :, lanes].reshape(shards * rest_rows, LANES).astype(jnp.float32)
                for k in range(slots):
                    rests[k, :, lanes] = jnp.concatenate([
                        spread[pl.ds(left * k + i, shards, stride=rest_rows), :] for i in range(left)
                    ], axis=0).astype(rests.dtype)

        left_side[:shards * body_rows] = main_ref[...].reshape(shards * body_rows, flat)
        left_side[shards * body_rows:] = rests[slot]
        sums[...] += jnp.dot(left_side[...], weights[...], preferred_element_type=jnp.float32)

        @pl.when(slot == slots - 1)
        def _():
            total = 0.5 * sums[...]
            full = total[:shards * body_rows].reshape(shards, body_rows, cols)
            folded = jnp.stack([
                total[shards * (body_rows + i):shards * (body_rows + i + 1)] for i in range(left)], axis=1)
            for b in range(main):
                lanes = slice(LANES * b, LANES * (b + 1))
                out[:, body_rows * b:body_rows * (b + 1), :] = full[:, :, lanes].astype(out.dtype)
                tail[:, left * b:left * (b + 1), :] = folded[:, :, lanes]
            at = left * main
            tail[:, at + strip + left:, :] = jnp.zeros((shards, tail_rows - at - strip - left, LANES), jnp.float32)
            for i in range(per):
                tail[:, at:at + strip, over * i:over * (i + 1)] = full[:, strip * i:strip * (i + 1), LANES * main:]
            tail[:, at + strip:at + strip + left, over:] = jnp.zeros((shards, left, LANES - over), jnp.float32)
            tail[:, at + strip:at + strip + left, :over] = folded[:, :, LANES * main:]
            out[:, body_rows * main:, :] = tail[...].astype(out.dtype)

    out_rows = body_rows * main + tail_rows
    return pl.pallas_call(
        body,
        grid=(slots,),
        in_specs=[
            pl.BlockSpec((shards, body_rows, flat), lambda k: (0, k, 0)),
            pl.BlockSpec((shards, rest_rows, flat), lambda k: (0, body_rows * slots // rest_rows, 0)),
            pl.BlockSpec((1, flat, cols), lambda k: (k, 0, 0)),
        ]
        + [pl.BlockSpec(memory_space=pltpu.VMEM) for other in others],
        out_specs=pl.BlockSpec((shards, out_rows, LANES), lambda k: (0, 0, 0)),
        out_shape=jax.ShapeDtypeStruct((shards, out_rows, LANES), gathered.dtype),
        scratch_shapes=[
            pltpu.VMEM((flat, cols), held.dtype),
            pltpu.VMEM((shards * pairs, flat), held.dtype),
            pltpu.VMEM((shards * rest_rows, LANES), jnp.float32),
            pltpu.VMEM((slots, shards * left, flat), held.dtype),
            pltpu.VMEM((shards * pairs, cols), jnp.float32),
            pltpu.VMEM((shards, tail_rows, LANES), jnp.float32),
        ],
        compiler_params=pltpu.CompilerParams(vmem_limit_bytes=VMEM_BYTES),
        cost_estimate=pl.CostEstimate(
            flops=2 * slots * shards * pairs * flat * cols,
            bytes_accessed=2 * gathered.size + 2 * held.size, transcendentals=0),
        name="contract",
    )(gathered, gathered, held, *others)


def padded_tail(body_rows, left, cols):
    main, over, per, _ = packed_rows(body_rows, cols)
    return -(-(left * main + body_rows // per + left) // 16) * 16


def add_pieces(pieces, body_rows, left, cols):
    main, over, per, _ = packed_rows(body_rows, cols)
    strip = body_rows // per

    def body(pieces_ref, out, scratch):
        total = jnp.sum(pieces_ref[...].astype(jnp.float32), axis=0)
        tail = total[body_rows * main:]
        at = left * main
        for b in range(main):
            lanes = slice(LANES * b, LANES * (b + 1))
            scratch[:body_rows, lanes] = total[body_rows * b:body_rows * (b + 1)]
            scratch[body_rows:, lanes] = tail[left * b:left * (b + 1)]
        for i in range(per):
            scratch[strip * i:strip * (i + 1), LANES * main:] = tail[at:at + strip, over * i:over * (i + 1)]
        scratch[body_rows:, LANES * main:] = tail[at + strip:at + strip + left, :over]
        out[...] = scratch[...].astype(out.dtype)

    return pl.pallas_call(
        body,
        out_shape=jax.ShapeDtypeStruct((body_rows + left, cols), pieces.dtype),
        scratch_shapes=[pltpu.VMEM((body_rows + left, cols), jnp.float32)],
        compiler_params=pltpu.CompilerParams(vmem_limit_bytes=VMEM_BYTES),
        name="add_pieces",
    )(pieces)


BODY_ROWS = 48
EARLY = 1


def local(t_amps, integrals, virt_irrep, tile_map):
    own_rows, c_count, virt_count = t_amps.shape
    own_cols = integrals.shape[2]
    assert c_count == TILE and own_cols == virt_count
    whole, split = len(WHOLE), len(SPLIT)
    place = jnp.stack([lax.axis_index("row"), lax.axis_index(("col", "depth"))]).astype(jnp.int32)

    own = tile_major(jnp.transpose(t_amps, (1, 0, 2)))
    mirrored = lax.all_to_all(own, "row", split_axis=0, concat_axis=0, tiled=True)
    sent_whole = take_tiles(integrals, place, virt_irrep, tile_map, 0, whole, 0, True)
    mirrored, sent_whole = lax.optimization_barrier((mirrored, sent_whole))
    part = antisymmetrize(own, mirrored, place, BODY_ROWS)
    part, sent_whole, place = lax.optimization_barrier((part, sent_whole, place))
    gathered = lax.all_gather(part, ("col", "depth"), axis=0, tiled=False)

    def exchange(offsets, tiles):
        moved = []
        for offset, tile in zip(offsets, tiles):
            if offset != (0, 0):
                moves = [(neighbour(r, offset, 1), r) for r in range(SIDE * SIDE)]
                tile = lax.ppermute(tile, "row", moves)
            moved.append(tile)
        return moved

    others = exchange(WHOLE, sent_whole)
    held = take_tiles(integrals, place, virt_irrep, tile_map, 0, whole, split, False)[0]
    held, place = lax.optimization_barrier((held, place))
    sent_split = take_tiles(integrals, place, virt_irrep, tile_map, whole, 0, split, True)
    others[:EARLY], sent_split = lax.optimization_barrier((others[:EARLY], sent_split))
    others = others + exchange(SPLIT, sent_split)
    result = contract(gathered, held, others, BODY_ROWS)
    pieces = lax.all_to_all(result, "row", split_axis=0, concat_axis=0, tiled=True)
    return add_pieces(pieces, BODY_ROWS, own_rows - BODY_ROWS, own_cols)


def solution(mesh):
    placed = (P(("col", "depth"), "row", None), P("row", None, ("col", "depth")), P(), P())
    return jax.shard_map(
        local, mesh=mesh, in_specs=placed, out_specs=P("row", ("col", "depth")), check_vma=False
    )
```

```python
import jax
import jax.numpy as jnp
import numpy as np
from jax import lax
from jax.experimental import pallas as pl
from jax.experimental.pallas import tpu as pltpu
from jax.sharding import PartitionSpec as P

TILE = 25
LANES = 128
WINDOW = 16
SIDE = 4
WHOLE = ((3, 2), (2, 1), (3, 3), (1, 3), (0, 1), (1, 0))
SPLIT = ((0, 2), (2, 0), (2, 2), (0, 0))
NOWHERE = -(1 << 20)
VMEM_BYTES = 52 * 1024 * 1024


def split_pairs(variant):
    chosen = [(u, v) for u in range(TILE) for v in range(u + 1, TILE)]
    middle = (TILE + 1) // 2
    if variant == 0:
        chosen += [(u, u) for u in range(middle)]
    elif variant == 1:
        chosen += [(u, u) for u in range(middle, TILE)]
    return chosen


def whole_pairs():
    return [(u, v) for u in range(TILE) for v in range(TILE)]


def padded_flat(count):
    return -(-count // LANES) * LANES


def row_targets(pairs, rows, swapped):
    target = np.full((rows, 1), NOWHERE, np.int32)
    for k, (u, v) in enumerate(pairs):
        target[k, 0] = v * 3 * WINDOW + u if swapped else u * 3 * WINDOW + v
    return target


def swap_row(flat):
    row = np.full((1, flat), NOWHERE, np.int32)
    for u, v in whole_pairs():
        row[0, v * TILE + u] = u * TILE + v
    return jnp.asarray(row)


def choice_rows(flat):
    rows = np.full((3, 1, flat // 2), NOWHERE, np.int32)
    for variant in range(3):
        for k, (u, v) in enumerate(split_pairs(variant)):
            rows[variant, 0, k] = u * TILE + v
    return jnp.asarray(rows)


def one_hot(row, count, dtype):
    places = lax.broadcasted_iota(jnp.int32, (count, row.shape[1]), 0)
    return jnp.where(places == row, 1.0, 0.0).astype(dtype)


def neighbour(row, offset, sign):
    y = (row // SIDE + sign * offset[0]) % SIDE
    x = (row % SIDE + sign * offset[1]) % SIDE
    return y * SIDE + x


def schedule(sign):
    others = np.zeros((SIDE * SIDE, len(WHOLE) + len(SPLIT)), np.int32)
    variants = np.zeros_like(others)
    for row in range(SIDE * SIDE):
        for k, offset in enumerate(WHOLE + SPLIT):
            other = neighbour(row, offset, sign)
            worker, source = (row, other) if sign == 1 else (other, row)
            others[row, k] = other
            variants[row, k] = 2 if offset == (0, 0) else int(worker > source)
    return jnp.asarray(others.ravel()), jnp.asarray(variants.ravel())


def antisymmetrize(own, mirrored, place, body_rows):
    tiles, pairs, flat = own.shape
    whole, split = len(WHOLE), len(SPLIT)
    slots = whole + split // 2
    left = pairs - body_rows
    padded = -(-pairs // 16) * 16

    def body(place_ref, places_ref, variants_ref, own_ref, mirrored_ref, swap_ref, choice_ref, out, stack, rest, tile):
        first = place_ref[0] * (whole + split)
        for k in range(whole + split):
            stack[padded * k:padded * k + pairs] = mirrored_ref[places_ref[first + k]]
        swap = one_hot(swap_ref[...], flat, own.dtype)
        swapped = jnp.dot(stack[...], swap, preferred_element_type=jnp.float32)

        def difference(k):
            return own_ref[places_ref[first + k]].astype(jnp.float32) - swapped[padded * k:padded * k + pairs]

        def store(slot, value):
            out[body_rows * slot:body_rows * (slot + 1)] = value[:body_rows].astype(own.dtype)
            rest[left * slot:left * (slot + 1)] = value[body_rows:]

        for k in range(whole):
            store(k, difference(k))
        for m in range(split // 2):
            ends = []
            for k in (whole + 2 * m, whole + 2 * m + 1):
                tile[:pairs] = difference(k).astype(own.dtype)
                choice = one_hot(choice_ref[variants_ref[first + k]], flat, own.dtype)
                ends.append(jnp.dot(tile[...], choice, preferred_element_type=jnp.float32)[:pairs])
            store(whole + m, jnp.concatenate(ends, axis=1))
        out[body_rows * slots:] = rest[...].astype(own.dtype)

    smem = pl.BlockSpec(memory_space=pltpu.SMEM)
    vmem = pl.BlockSpec(memory_space=pltpu.VMEM)
    return pl.pallas_call(
        body,
        in_specs=[smem, smem, smem, vmem, vmem, vmem, vmem],
        out_shape=jax.ShapeDtypeStruct((slots * pairs, flat), own.dtype),
        scratch_shapes=[
            pltpu.VMEM(((whole + split) * padded, flat), own.dtype),
            pltpu.VMEM((left * slots, flat), jnp.float32),
            pltpu.VMEM((padded, flat), own.dtype),
        ],
        compiler_params=pltpu.CompilerParams(vmem_limit_bytes=VMEM_BYTES),
        name="antisymmetrize",
    )(place, *schedule(1), own, mirrored, swap_row(flat), choice_rows(flat))


def packed_rows(rows, cols):
    main, over = cols // LANES, cols % LANES
    per = LANES // over
    return main, over, per, -(-rows // per // 16) * 16


def take_tiles(integrals, place, irrep, tile_map, base, whole, split, swapped):
    c_count, virt, cols = integrals.shape
    flat = padded_flat(TILE * TILE)
    half = flat // 2
    blocks = virt // WINDOW
    span = 3 * WINDOW
    whole_target = jnp.asarray(row_targets(whole_pairs(), flat, swapped))
    split_target = jnp.asarray(np.stack([row_targets(split_pairs(v), half, swapped) for v in range(3)]))
    main, over, per, _ = packed_rows(flat, cols)
    sizes = [flat] * whole + [half] * split
    stripes = [max(-(-rows // per), 80) for rows in sizes]

    slots = len(WHOLE) + len(SPLIT)

    def body(place_ref, others_ref, variants_ref, irrep_ref, kept_ref,
             r0, r1, r2, column_ref, whole_ref, split_ref, v0, v1, v2, *refs):
        outs, slab = refs[:-1], refs[-1]
        s = pl.program_id(0)
        row, shard = place_ref[0], place_ref[1]
        entry = row * slots + base + s
        other = others_ref[entry]
        offset = other * TILE % WINDOW
        dropped = jnp.where(kept_ref[row, other] != 0, 0, 1 << 20)
        for q, (r, v) in enumerate(((r0, v0), (r1, v1), (r2, v2))):
            code = jnp.bitwise_xor(r[...], column_ref[...])
            for c in range(c_count):
                wanted = jnp.bitwise_xor(irrep_ref[row * c_count + c], irrep_ref[shard]) + dropped
                kept = jnp.where(code == wanted, v[c].astype(jnp.float32), 0.0)
                slab[span * c + WINDOW * q:span * c + WINDOW * (q + 1), :] = kept.astype(integrals.dtype)

        def pick(target):
            place = lax.broadcasted_iota(jnp.int32, (target.shape[0], span * c_count), 1)
            chosen = jnp.where(place == target + offset, 1.0, 0.0).astype(integrals.dtype)
            return jnp.dot(chosen, slab[...], preferred_element_type=jnp.float32).astype(integrals.dtype)

        def pack(out, rows, stripe, value):
            for b in range(main):
                out[rows * b:rows * (b + 1), :] = value[:, LANES * b:LANES * (b + 1)]
            strips = [value[stripe * i:stripe * (i + 1), LANES * main:] for i in range(rows // stripe)]
            strips += [jnp.zeros_like(strips[0])] * (per - len(strips))
            out[rows * main:, :] = jnp.concatenate(strips, axis=1)

        @pl.when(s < whole)
        def _():
            value = pick(whole_ref[...])
            if swapped:
                for k in range(whole):
                    @pl.when(s == k)
                    def _(k=k):
                        pack(outs[k], flat, stripes[k], value)
            else:
                outs[0][0] = value

        @pl.when(s >= whole)
        def _():
            value = pick(split_ref[variants_ref[entry]])
            for k in range(whole, whole + split):
                @pl.when(s == k)
                def _(k=k):
                    if swapped:
                        pack(outs[k], half, stripes[k], value)
                    else:
                        low = half * ((k - whole) % 2)
                        outs[0][0, low:low + half, :] = value

    def block(q, s, place, others):
        start = others[place[0] * slots + base + s] * TILE
        return jnp.minimum(start // WINDOW + q, blocks - 1)

    def window(q):
        return lambda s, place, others, *_: (0, block(q, s, place, others), 0)

    def code_window(q):
        return lambda s, place, others, *_: (block(q, s, place, others), 0)

    fixed = lambda rank: (lambda s, *_: (0,) * rank)
    if swapped:
        shapes = [(main * rows + stripe, LANES) for rows, stripe in zip(sizes, stripes)]
        out_specs = [pl.BlockSpec(shape, fixed(2)) for shape in shapes]
        out_shape = [jax.ShapeDtypeStruct(shape, integrals.dtype) for shape in shapes]
    else:
        out_specs = [pl.BlockSpec(
            (1, flat, cols), lambda s, *_: (jnp.where(s < whole, s, whole + (s - whole) // 2), 0, 0))]
        out_shape = [jax.ShapeDtypeStruct((whole + split // 2, flat, cols), integrals.dtype)]
    return pl.pallas_call(
        body,
        grid_spec=pltpu.PrefetchScalarGridSpec(
            num_scalar_prefetch=5,
            grid=(whole + split,),
            in_specs=[pl.BlockSpec((WINDOW, 1), code_window(q)) for q in range(3)]
            + [
                pl.BlockSpec((1, cols), fixed(2)),
                pl.BlockSpec((flat, 1), fixed(2)),
                pl.BlockSpec((3, half, 1), fixed(3)),
            ]
            + [pl.BlockSpec((c_count, WINDOW, cols), window(q)) for q in range(3)],
            out_specs=out_specs,
            scratch_shapes=[pltpu.VMEM((span * c_count, cols), integrals.dtype)],
        ),
        out_shape=out_shape,
        compiler_params=pltpu.CompilerParams(vmem_limit_bytes=VMEM_BYTES),
        cost_estimate=pl.CostEstimate(
            flops=2 * (whole + split // 2) * flat * span * c_count * cols,
            bytes_accessed=2 * (whole + split) * span * c_count * cols, transcendentals=0),
        name="take_swapped_tiles" if swapped else "take_own_tiles",
    )(place, *schedule(-1 if swapped else 1), irrep, tile_map, *[irrep[:, None]] * 3, irrep[None, :],
      whole_target, split_target, integrals, integrals, integrals)


def tile_major(t):
    c_count, pairs, virt = t.shape
    tiles = virt // TILE
    flat = -(-c_count * TILE // LANES) * LANES

    def body(t_ref, out_ref):
        for j in range(tiles):
            parts = [t_ref[c, :, TILE * j:TILE * (j + 1)] for c in range(c_count)]
            parts.append(jnp.zeros((pairs, flat - c_count * TILE), t.dtype))
            out_ref[j] = jnp.concatenate(parts, axis=1)

    return pl.pallas_call(
        body,
        out_shape=jax.ShapeDtypeStruct((tiles, pairs, flat), t.dtype),
        compiler_params=pltpu.CompilerParams(vmem_limit_bytes=VMEM_BYTES),
        name="tile_major",
    )(t)


def less(held_ref, out, low, count, other):
    cols = held_ref.shape[2]
    main, over, _, _ = packed_rows(count, cols)
    stripe = other.shape[0] - main * count
    for b in range(main):
        lanes = slice(LANES * b, LANES * (b + 1))
        out[low:low + count, lanes] = (
            held_ref[0, low:low + count, lanes].astype(jnp.float32)
            - other[count * b:count * (b + 1), :].astype(jnp.float32)
        ).astype(out.dtype)
    last = other[count * main:, :].astype(jnp.float32)
    for i in range(count // stripe):
        at = slice(low + stripe * i, low + stripe * (i + 1))
        out[at, LANES * main:] = (
            held_ref[0, at, LANES * main:].astype(jnp.float32) - last[:, over * i:over * (i + 1)]
        ).astype(out.dtype)


def subtract_tiles(held, others):
    slots, flat, cols = held.shape

    def body(held_ref, *refs):
        others_ref, out = refs[:-1], refs[-1]
        for k in range(len(others)):
            @pl.when(pl.program_id(0) == k)
            def _(k=k):
                less(held_ref, out.at[0], 0, flat, others_ref[k])

    tile = pl.BlockSpec((1, flat, cols), lambda k: (k, 0, 0))
    return pl.pallas_call(
        body,
        grid=(len(others),),
        in_specs=[tile] + [pl.BlockSpec(memory_space=pltpu.VMEM) for other in others],
        out_specs=tile,
        out_shape=jax.ShapeDtypeStruct(held.shape, held.dtype),
        input_output_aliases={0: 0},
        compiler_params=pltpu.CompilerParams(vmem_limit_bytes=VMEM_BYTES),
        cost_estimate=pl.CostEstimate(
            flops=len(others) * flat * cols, bytes_accessed=6 * len(others) * flat * cols, transcendentals=0),
        name="subtract_tiles",
    )(held, *others)


def contract(gathered, held, others, ready, body_rows):
    shards, rows, flat = gathered.shape
    slots, _, cols = held.shape
    pairs = rows // slots
    left = pairs - body_rows
    rest_rows = left * slots
    whole = len(WHOLE)
    half = flat // 2
    main, over, per, _ = packed_rows(flat, cols)
    strip = body_rows // per
    tail_rows = padded_tail(body_rows, left, cols)

    def body(main_ref, rest_ref, held_ref, *refs):
        others_ref, (out, weights, left_side, spread, rests, sums, tail) = refs[:-7], refs[-7:]
        slot = pl.program_id(0)

        @pl.when(slot < ready)
        def _():
            weights[...] = held_ref[0]

        for k in range(ready, slots):
            @pl.when(slot == k)
            def _(k=k):
                if k < whole:
                    less(held_ref, weights, 0, flat, others_ref[k - ready])
                else:
                    less(held_ref, weights, 0, half, others_ref[whole - ready + 2 * (k - whole)])
                    less(held_ref, weights, half, half, others_ref[whole - ready + 2 * (k - whole) + 1])

        @pl.when(slot == 0)
        def _():
            sums[...] = jnp.zeros(sums.shape, jnp.float32)
            for b in range(flat // LANES):
                lanes = slice(LANES * b, LANES * (b + 1))
                spread[...] = rest_ref[:, :, lanes].reshape(shards * rest_rows, LANES).astype(jnp.float32)
                for k in range(slots):
                    rests[k, :, lanes] = jnp.concatenate([
                        spread[pl.ds(left * k + i, shards, stride=rest_rows), :] for i in range(left)
                    ], axis=0).astype(rests.dtype)

        left_side[:shards * body_rows] = main_ref[...].reshape(shards * body_rows, flat)
        left_side[shards * body_rows:] = rests[slot]
        sums[...] += jnp.dot(left_side[...], weights[...], preferred_element_type=jnp.float32)

        @pl.when(slot == slots - 1)
        def _():
            total = 0.5 * sums[...]
            full = total[:shards * body_rows].reshape(shards, body_rows, cols)
            folded = jnp.stack([
                total[shards * (body_rows + i):shards * (body_rows + i + 1)] for i in range(left)], axis=1)
            for b in range(main):
                lanes = slice(LANES * b, LANES * (b + 1))
                out[:, body_rows * b:body_rows * (b + 1), :] = full[:, :, lanes].astype(out.dtype)
                tail[:, left * b:left * (b + 1), :] = folded[:, :, lanes]
            at = left * main
            tail[:, at + strip + left:, :] = jnp.zeros((shards, tail_rows - at - strip - left, LANES), jnp.float32)
            for i in range(per):
                tail[:, at:at + strip, over * i:over * (i + 1)] = full[:, strip * i:strip * (i + 1), LANES * main:]
            tail[:, at + strip:at + strip + left, over:] = jnp.zeros((shards, left, LANES - over), jnp.float32)
            tail[:, at + strip:at + strip + left, :over] = folded[:, :, LANES * main:]
            out[:, body_rows * main:, :] = tail[...].astype(out.dtype)

    out_rows = body_rows * main + tail_rows
    return pl.pallas_call(
        body,
        grid=(slots,),
        in_specs=[
            pl.BlockSpec((shards, body_rows, flat), lambda k: (0, k, 0)),
            pl.BlockSpec((shards, rest_rows, flat), lambda k: (0, body_rows * slots // rest_rows, 0)),
            pl.BlockSpec((1, flat, cols), lambda k: (k, 0, 0)),
        ]
        + [pl.BlockSpec(memory_space=pltpu.VMEM) for other in others],
        out_specs=pl.BlockSpec((shards, out_rows, LANES), lambda k: (0, 0, 0)),
        out_shape=jax.ShapeDtypeStruct((shards, out_rows, LANES), gathered.dtype),
        scratch_shapes=[
            pltpu.VMEM((flat, cols), held.dtype),
            pltpu.VMEM((shards * pairs, flat), held.dtype),
            pltpu.VMEM((shards * rest_rows, LANES), jnp.float32),
            pltpu.VMEM((slots, shards * left, flat), held.dtype),
            pltpu.VMEM((shards * pairs, cols), jnp.float32),
            pltpu.VMEM((shards, tail_rows, LANES), jnp.float32),
        ],
        compiler_params=pltpu.CompilerParams(vmem_limit_bytes=VMEM_BYTES),
        cost_estimate=pl.CostEstimate(
            flops=2 * slots * shards * pairs * flat * cols,
            bytes_accessed=2 * gathered.size + 2 * held.size, transcendentals=0),
        name="contract",
    )(gathered, gathered, held, *others)


def padded_tail(body_rows, left, cols):
    main, over, per, _ = packed_rows(body_rows, cols)
    return -(-(left * main + body_rows // per + left) // 16) * 16


def add_pieces(pieces, body_rows, left, cols):
    main, over, per, _ = packed_rows(body_rows, cols)
    strip = body_rows // per

    def body(pieces_ref, out, scratch):
        total = jnp.sum(pieces_ref[...].astype(jnp.float32), axis=0)
        tail = total[body_rows * main:]
        at = left * main
        for b in range(main):
            lanes = slice(LANES * b, LANES * (b + 1))
            scratch[:body_rows, lanes] = total[body_rows * b:body_rows * (b + 1)]
            scratch[body_rows:, lanes] = tail[left * b:left * (b + 1)]
        for i in range(per):
            scratch[strip * i:strip * (i + 1), LANES * main:] = tail[at:at + strip, over * i:over * (i + 1)]
        scratch[body_rows:, LANES * main:] = tail[at + strip:at + strip + left, :over]
        out[...] = scratch[...].astype(out.dtype)

    return pl.pallas_call(
        body,
        out_shape=jax.ShapeDtypeStruct((body_rows + left, cols), pieces.dtype),
        scratch_shapes=[pltpu.VMEM((body_rows + left, cols), jnp.float32)],
        compiler_params=pltpu.CompilerParams(vmem_limit_bytes=VMEM_BYTES),
        name="add_pieces",
    )(pieces)


BODY_ROWS = 48
EARLY = 1
READY = 3


def local(t_amps, integrals, virt_irrep, tile_map):
    own_rows, c_count, virt_count = t_amps.shape
    own_cols = integrals.shape[2]
    assert c_count == TILE and own_cols == virt_count
    whole, split = len(WHOLE), len(SPLIT)
    place = jnp.stack([lax.axis_index("row"), lax.axis_index(("col", "depth"))]).astype(jnp.int32)

    own = tile_major(jnp.transpose(t_amps, (1, 0, 2)))
    mirrored = lax.all_to_all(own, "row", split_axis=0, concat_axis=0, tiled=True)
    sent_whole = take_tiles(integrals, place, virt_irrep, tile_map, 0, whole, 0, True)
    mirrored, sent_whole = lax.optimization_barrier((mirrored, sent_whole))
    part = antisymmetrize(own, mirrored, place, BODY_ROWS)
    part, sent_whole, place = lax.optimization_barrier((part, sent_whole, place))
    gathered = lax.all_gather(part, ("col", "depth"), axis=0, tiled=False)

    def exchange(offsets, tiles):
        moved = []
        for offset, tile in zip(offsets, tiles):
            if offset != (0, 0):
                moves = [(neighbour(r, offset, 1), r) for r in range(SIDE * SIDE)]
                tile = lax.ppermute(tile, "row", moves)
            moved.append(tile)
        return moved

    others = exchange(WHOLE, sent_whole)
    held = take_tiles(integrals, place, virt_irrep, tile_map, 0, whole, split, False)[0]
    held, place = lax.optimization_barrier((held, place))
    sent_split = take_tiles(integrals, place, virt_irrep, tile_map, whole, 0, split, True)
    others[:EARLY], sent_split = lax.optimization_barrier((others[:EARLY], sent_split))
    others = others + exchange(SPLIT, sent_split)
    held = subtract_tiles(held, others[:READY])
    result = contract(gathered, held, others[READY:], READY, BODY_ROWS)
    pieces = lax.all_to_all(result, "row", split_axis=0, concat_axis=0, tiled=True)
    return add_pieces(pieces, BODY_ROWS, own_rows - BODY_ROWS, own_cols)


def solution(mesh):
    placed = (P(("col", "depth"), "row", None), P("row", None, ("col", "depth")), P(), P())
    return jax.shard_map(
        local, mesh=mesh, in_specs=placed, out_specs=P("row", ("col", "depth")), check_vma=False
    )
```

```python
import jax
import jax.numpy as jnp
import numpy as np
from jax import lax
from jax.experimental import pallas as pl
from jax.experimental.pallas import tpu as pltpu
from jax.sharding import PartitionSpec as P

TILE = 25
LANES = 128
WINDOW = 16
SIDE = 4
WHOLE = ((3, 2), (2, 1), (3, 3), (1, 3), (0, 1), (1, 0))
SPLIT = ((0, 2), (2, 0), (2, 2), (0, 0))
NOWHERE = -(1 << 20)
VMEM_BYTES = 52 * 1024 * 1024


def split_pairs(variant):
    chosen = [(u, v) for u in range(TILE) for v in range(u + 1, TILE)]
    middle = (TILE + 1) // 2
    if variant == 0:
        chosen += [(u, u) for u in range(middle)]
    elif variant == 1:
        chosen += [(u, u) for u in range(middle, TILE)]
    return chosen


def whole_pairs():
    return [(u, v) for u in range(TILE) for v in range(TILE)]


def padded_flat(count):
    return -(-count // LANES) * LANES


def row_targets(pairs, rows, swapped):
    target = np.full((rows, 1), NOWHERE, np.int32)
    for k, (u, v) in enumerate(pairs):
        target[k, 0] = v * 3 * WINDOW + u if swapped else u * 3 * WINDOW + v
    return target


def swap_row(flat):
    row = np.full((1, flat), NOWHERE, np.int32)
    for u, v in whole_pairs():
        row[0, v * TILE + u] = u * TILE + v
    return jnp.asarray(row)


def choice_rows(flat):
    rows = np.full((3, 1, flat // 2), NOWHERE, np.int32)
    for variant in range(3):
        for k, (u, v) in enumerate(split_pairs(variant)):
            rows[variant, 0, k] = u * TILE + v
    return jnp.asarray(rows)


def one_hot(row, count, dtype):
    places = lax.broadcasted_iota(jnp.int32, (count, row.shape[1]), 0)
    return jnp.where(places == row, 1.0, 0.0).astype(dtype)


def neighbour(row, offset, sign):
    y = (row // SIDE + sign * offset[0]) % SIDE
    x = (row % SIDE + sign * offset[1]) % SIDE
    return y * SIDE + x


def schedule(sign):
    others = np.zeros((SIDE * SIDE, len(WHOLE) + len(SPLIT)), np.int32)
    variants = np.zeros_like(others)
    for row in range(SIDE * SIDE):
        for k, offset in enumerate(WHOLE + SPLIT):
            other = neighbour(row, offset, sign)
            worker, source = (row, other) if sign == 1 else (other, row)
            others[row, k] = other
            variants[row, k] = 2 if offset == (0, 0) else int(worker > source)
    return jnp.asarray(others.ravel()), jnp.asarray(variants.ravel())


def antisymmetrize(own, mirrored, place, body_rows):
    tiles, pairs, flat = own.shape
    whole, split = len(WHOLE), len(SPLIT)
    slots = whole + split // 2
    left = pairs - body_rows
    padded = -(-pairs // 16) * 16

    def body(place_ref, places_ref, variants_ref, own_ref, mirrored_ref, swap_ref, choice_ref, out, stack, rest, tile):
        first = place_ref[0] * (whole + split)
        for k in range(whole + split):
            stack[padded * k:padded * k + pairs] = mirrored_ref[places_ref[first + k]]
        swap = one_hot(swap_ref[...], flat, own.dtype)
        swapped = jnp.dot(stack[...], swap, preferred_element_type=jnp.float32)

        def difference(k):
            return own_ref[places_ref[first + k]].astype(jnp.float32) - swapped[padded * k:padded * k + pairs]

        def store(slot, value):
            out[body_rows * slot:body_rows * (slot + 1)] = value[:body_rows].astype(own.dtype)
            rest[left * slot:left * (slot + 1)] = value[body_rows:]

        for k in range(whole):
            store(k, difference(k))
        for m in range(split // 2):
            ends = []
            for k in (whole + 2 * m, whole + 2 * m + 1):
                tile[:pairs] = difference(k).astype(own.dtype)
                choice = one_hot(choice_ref[variants_ref[first + k]], flat, own.dtype)
                ends.append(jnp.dot(tile[...], choice, preferred_element_type=jnp.float32)[:pairs])
            store(whole + m, jnp.concatenate(ends, axis=1))
        out[body_rows * slots:] = rest[...].astype(own.dtype)

    smem = pl.BlockSpec(memory_space=pltpu.SMEM)
    vmem = pl.BlockSpec(memory_space=pltpu.VMEM)
    return pl.pallas_call(
        body,
        in_specs=[smem, smem, smem, vmem, vmem, vmem, vmem],
        out_shape=jax.ShapeDtypeStruct((slots * pairs, flat), own.dtype),
        scratch_shapes=[
            pltpu.VMEM(((whole + split) * padded, flat), own.dtype),
            pltpu.VMEM((left * slots, flat), jnp.float32),
            pltpu.VMEM((padded, flat), own.dtype),
        ],
        compiler_params=pltpu.CompilerParams(vmem_limit_bytes=VMEM_BYTES),
        name="antisymmetrize",
    )(place, *schedule(1), own, mirrored, swap_row(flat), choice_rows(flat))


def packed_rows(rows, cols):
    main, over = cols // LANES, cols % LANES
    per = LANES // over
    return main, over, per, -(-rows // per // 16) * 16


def take_tiles(integrals, place, irrep, tile_map, base, whole, split, swapped):
    c_count, virt, cols = integrals.shape
    flat = padded_flat(TILE * TILE)
    half = flat // 2
    blocks = virt // WINDOW
    span = 3 * WINDOW
    whole_target = jnp.asarray(row_targets(whole_pairs(), flat, swapped))
    split_target = jnp.asarray(np.stack([row_targets(split_pairs(v), half, swapped) for v in range(3)]))
    main, over, per, _ = packed_rows(flat, cols)
    sizes = [flat] * whole + [half] * split
    stripes = [max(-(-rows // per), 80) for rows in sizes]

    slots = len(WHOLE) + len(SPLIT)

    def body(place_ref, others_ref, variants_ref, irrep_ref, kept_ref,
             r0, r1, r2, column_ref, whole_ref, split_ref, v0, v1, v2, *refs):
        outs, slab = refs[:-1], refs[-1]
        s = pl.program_id(0)
        row, shard = place_ref[0], place_ref[1]
        entry = row * slots + base + s
        other = others_ref[entry]
        offset = other * TILE % WINDOW
        dropped = jnp.where(kept_ref[row, other] != 0, 0, 1 << 20)
        for q, (r, v) in enumerate(((r0, v0), (r1, v1), (r2, v2))):
            code = jnp.bitwise_xor(r[...], column_ref[...])
            for c in range(c_count):
                wanted = jnp.bitwise_xor(irrep_ref[row * c_count + c], irrep_ref[shard]) + dropped
                kept = jnp.where(code == wanted, v[c].astype(jnp.float32), 0.0)
                slab[span * c + WINDOW * q:span * c + WINDOW * (q + 1), :] = kept.astype(integrals.dtype)

        def pick(target):
            place = lax.broadcasted_iota(jnp.int32, (target.shape[0], span * c_count), 1)
            chosen = jnp.where(place == target + offset, 1.0, 0.0).astype(integrals.dtype)
            return jnp.dot(chosen, slab[...], preferred_element_type=jnp.float32).astype(integrals.dtype)

        def pack(out, rows, stripe, value):
            for b in range(main):
                out[rows * b:rows * (b + 1), :] = value[:, LANES * b:LANES * (b + 1)]
            strips = [value[stripe * i:stripe * (i + 1), LANES * main:] for i in range(rows // stripe)]
            strips += [jnp.zeros_like(strips[0])] * (per - len(strips))
            out[rows * main:, :] = jnp.concatenate(strips, axis=1)

        @pl.when(s < whole)
        def _():
            value = pick(whole_ref[...])
            if swapped:
                for k in range(whole):
                    @pl.when(s == k)
                    def _(k=k):
                        pack(outs[k], flat, stripes[k], value)
            else:
                outs[0][0] = value

        @pl.when(s >= whole)
        def _():
            value = pick(split_ref[variants_ref[entry]])
            for k in range(whole, whole + split):
                @pl.when(s == k)
                def _(k=k):
                    if swapped:
                        pack(outs[k], half, stripes[k], value)
                    else:
                        low = half * ((k - whole) % 2)
                        outs[0][0, low:low + half, :] = value

    def block(q, s, place, others):
        start = others[place[0] * slots + base + s] * TILE
        return jnp.minimum(start // WINDOW + q, blocks - 1)

    def window(q):
        return lambda s, place, others, *_: (0, block(q, s, place, others), 0)

    def code_window(q):
        return lambda s, place, others, *_: (block(q, s, place, others), 0)

    fixed = lambda rank: (lambda s, *_: (0,) * rank)
    if swapped:
        shapes = [(main * rows + stripe, LANES) for rows, stripe in zip(sizes, stripes)]
        out_specs = [pl.BlockSpec(shape, fixed(2)) for shape in shapes]
        out_shape = [jax.ShapeDtypeStruct(shape, integrals.dtype) for shape in shapes]
    else:
        out_specs = [pl.BlockSpec(
            (1, flat, cols), lambda s, *_: (jnp.where(s < whole, s, whole + (s - whole) // 2), 0, 0))]
        out_shape = [jax.ShapeDtypeStruct((whole + split // 2, flat, cols), integrals.dtype)]
    return pl.pallas_call(
        body,
        grid_spec=pltpu.PrefetchScalarGridSpec(
            num_scalar_prefetch=5,
            grid=(whole + split,),
            in_specs=[pl.BlockSpec((WINDOW, 1), code_window(q)) for q in range(3)]
            + [
                pl.BlockSpec((1, cols), fixed(2)),
                pl.BlockSpec((flat, 1), fixed(2)),
                pl.BlockSpec((3, half, 1), fixed(3)),
            ]
            + [pl.BlockSpec((c_count, WINDOW, cols), window(q)) for q in range(3)],
            out_specs=out_specs,
            scratch_shapes=[pltpu.VMEM((span * c_count, cols), integrals.dtype)],
        ),
        out_shape=out_shape,
        compiler_params=pltpu.CompilerParams(vmem_limit_bytes=VMEM_BYTES),
        cost_estimate=pl.CostEstimate(
            flops=2 * (whole + split // 2) * flat * span * c_count * cols,
            bytes_accessed=2 * (whole + split) * span * c_count * cols, transcendentals=0),
        name="take_swapped_tiles" if swapped else "take_own_tiles",
    )(place, *schedule(-1 if swapped else 1), irrep, tile_map, *[irrep[:, None]] * 3, irrep[None, :],
      whole_target, split_target, integrals, integrals, integrals)


def tile_major(t):
    c_count, pairs, virt = t.shape
    tiles = virt // TILE
    flat = -(-c_count * TILE // LANES) * LANES

    def body(t_ref, out_ref):
        for j in range(tiles):
            parts = [t_ref[c, :, TILE * j:TILE * (j + 1)] for c in range(c_count)]
            parts.append(jnp.zeros((pairs, flat - c_count * TILE), t.dtype))
            out_ref[j] = jnp.concatenate(parts, axis=1)

    return pl.pallas_call(
        body,
        out_shape=jax.ShapeDtypeStruct((tiles, pairs, flat), t.dtype),
        compiler_params=pltpu.CompilerParams(vmem_limit_bytes=VMEM_BYTES),
        name="tile_major",
    )(t)


def less(held_ref, out, low, count, other):
    cols = held_ref.shape[2]
    main, over, _, _ = packed_rows(count, cols)
    stripe = other.shape[0] - main * count
    for b in range(main):
        lanes = slice(LANES * b, LANES * (b + 1))
        out[low:low + count, lanes] = (
            held_ref[0, low:low + count, lanes].astype(jnp.float32)
            - other[count * b:count * (b + 1), :].astype(jnp.float32)
        ).astype(out.dtype)
    last = other[count * main:, :].astype(jnp.float32)
    for i in range(count // stripe):
        at = slice(low + stripe * i, low + stripe * (i + 1))
        out[at, LANES * main:] = (
            held_ref[0, at, LANES * main:].astype(jnp.float32) - last[:, over * i:over * (i + 1)]
        ).astype(out.dtype)


def subtract_tiles(held, others):
    slots, flat, cols = held.shape

    def body(held_ref, *refs):
        others_ref, out = refs[:-1], refs[-1]
        for k in range(len(others)):
            @pl.when(pl.program_id(0) == k)
            def _(k=k):
                less(held_ref, out.at[0], 0, flat, others_ref[k])

    tile = pl.BlockSpec((1, flat, cols), lambda k: (k, 0, 0))
    return pl.pallas_call(
        body,
        grid=(len(others),),
        in_specs=[tile] + [pl.BlockSpec(memory_space=pltpu.VMEM) for other in others],
        out_specs=tile,
        out_shape=jax.ShapeDtypeStruct(held.shape, held.dtype),
        input_output_aliases={0: 0},
        compiler_params=pltpu.CompilerParams(vmem_limit_bytes=VMEM_BYTES),
        cost_estimate=pl.CostEstimate(
            flops=len(others) * flat * cols, bytes_accessed=6 * len(others) * flat * cols, transcendentals=0),
        name="subtract_tiles",
    )(held, *others)


def contract(gathered, held, others, ready, body_rows):
    shards, rows, flat = gathered.shape
    slots, _, cols = held.shape
    pairs = rows // slots
    left = pairs - body_rows
    rest_rows = left * slots
    whole = len(WHOLE)
    half = flat // 2
    main, over, per, _ = packed_rows(flat, cols)
    strip = body_rows // per
    tail_rows = padded_tail(body_rows, left, cols)

    def body(main_ref, rest_ref, held_ref, *refs):
        others_ref, (out, weights, left_side, spread, rests, sums, tail) = refs[:-7], refs[-7:]
        slot = pl.program_id(0)

        @pl.when(slot < ready)
        def _():
            weights[...] = held_ref[0]

        for k in range(ready, slots):
            @pl.when(slot == k)
            def _(k=k):
                if k < whole:
                    less(held_ref, weights, 0, flat, others_ref[k - ready])
                else:
                    less(held_ref, weights, 0, half, others_ref[whole - ready + 2 * (k - whole)])
                    less(held_ref, weights, half, half, others_ref[whole - ready + 2 * (k - whole) + 1])

        @pl.when(slot == 0)
        def _():
            sums[...] = jnp.zeros(sums.shape, jnp.float32)
            for b in range(flat // LANES):
                lanes = slice(LANES * b, LANES * (b + 1))
                spread[...] = rest_ref[:, :, lanes].reshape(shards * rest_rows, LANES).astype(jnp.float32)
                for k in range(slots):
                    rests[k, :, lanes] = jnp.concatenate([
                        spread[pl.ds(left * k + i, shards, stride=rest_rows), :] for i in range(left)
                    ], axis=0).astype(rests.dtype)

        left_side[:shards * body_rows] = main_ref[...].reshape(shards * body_rows, flat)
        left_side[shards * body_rows:] = rests[slot]
        sums[...] += jnp.dot(left_side[...], weights[...], preferred_element_type=jnp.float32)

        @pl.when(slot == slots - 1)
        def _():
            total = 0.5 * sums[...]
            full = total[:shards * body_rows].reshape(shards, body_rows, cols)
            folded = jnp.stack([
                total[shards * (body_rows + i):shards * (body_rows + i + 1)] for i in range(left)], axis=1)
            for b in range(main):
                lanes = slice(LANES * b, LANES * (b + 1))
                out[:, body_rows * b:body_rows * (b + 1), :] = full[:, :, lanes].astype(out.dtype)
                tail[:, left * b:left * (b + 1), :] = folded[:, :, lanes]
            at = left * main
            tail[:, at + strip + left:, :] = jnp.zeros((shards, tail_rows - at - strip - left, LANES), jnp.float32)
            for i in range(per):
                tail[:, at:at + strip, over * i:over * (i + 1)] = full[:, strip * i:strip * (i + 1), LANES * main:]
            tail[:, at + strip:at + strip + left, over:] = jnp.zeros((shards, left, LANES - over), jnp.float32)
            tail[:, at + strip:at + strip + left, :over] = folded[:, :, LANES * main:]
            out[:, body_rows * main:, :] = tail[...].astype(out.dtype)

    out_rows = body_rows * main + tail_rows
    return pl.pallas_call(
        body,
        grid=(slots,),
        in_specs=[
            pl.BlockSpec((shards, body_rows, flat), lambda k: (0, k, 0)),
            pl.BlockSpec((shards, rest_rows, flat), lambda k: (0, body_rows * slots // rest_rows, 0)),
            pl.BlockSpec((1, flat, cols), lambda k: (k, 0, 0)),
        ]
        + [pl.BlockSpec(memory_space=pltpu.VMEM) for other in others],
        out_specs=pl.BlockSpec((shards, out_rows, LANES), lambda k: (0, 0, 0)),
        out_shape=jax.ShapeDtypeStruct((shards, out_rows, LANES), gathered.dtype),
        scratch_shapes=[
            pltpu.VMEM((flat, cols), held.dtype),
            pltpu.VMEM((shards * pairs, flat), held.dtype),
            pltpu.VMEM((shards * rest_rows, LANES), jnp.float32),
            pltpu.VMEM((slots, shards * left, flat), held.dtype),
            pltpu.VMEM((shards * pairs, cols), jnp.float32),
            pltpu.VMEM((shards, tail_rows, LANES), jnp.float32),
        ],
        compiler_params=pltpu.CompilerParams(vmem_limit_bytes=VMEM_BYTES),
        cost_estimate=pl.CostEstimate(
            flops=2 * slots * shards * pairs * flat * cols,
            bytes_accessed=2 * gathered.size + 2 * held.size, transcendentals=0),
        name="contract",
    )(gathered, gathered, held, *others)


def padded_tail(body_rows, left, cols):
    main, over, per, _ = packed_rows(body_rows, cols)
    return -(-(left * main + body_rows // per + left) // 16) * 16


def add_pieces(pieces, body_rows, left, cols):
    main, over, per, _ = packed_rows(body_rows, cols)
    strip = body_rows // per

    def body(pieces_ref, out, scratch):
        total = jnp.sum(pieces_ref[...].astype(jnp.float32), axis=0)
        tail = total[body_rows * main:]
        at = left * main
        for b in range(main):
            lanes = slice(LANES * b, LANES * (b + 1))
            scratch[:body_rows, lanes] = total[body_rows * b:body_rows * (b + 1)]
            scratch[body_rows:, lanes] = tail[left * b:left * (b + 1)]
        for i in range(per):
            scratch[strip * i:strip * (i + 1), LANES * main:] = tail[at:at + strip, over * i:over * (i + 1)]
        scratch[body_rows:, LANES * main:] = tail[at + strip:at + strip + left, :over]
        out[...] = scratch[...].astype(out.dtype)

    return pl.pallas_call(
        body,
        out_shape=jax.ShapeDtypeStruct((body_rows + left, cols), pieces.dtype),
        scratch_shapes=[pltpu.VMEM((body_rows + left, cols), jnp.float32)],
        compiler_params=pltpu.CompilerParams(vmem_limit_bytes=VMEM_BYTES),
        name="add_pieces",
    )(pieces)


BODY_ROWS = 48
EARLY = 1
READY = 3


def local(t_amps, integrals, virt_irrep, tile_map):
    own_rows, c_count, virt_count = t_amps.shape
    own_cols = integrals.shape[2]
    assert c_count == TILE and own_cols == virt_count
    whole, split = len(WHOLE), len(SPLIT)
    place = jnp.stack([lax.axis_index("row"), lax.axis_index(("col", "depth"))]).astype(jnp.int32)

    own = tile_major(jnp.transpose(t_amps, (1, 0, 2)))
    mirrored = lax.all_to_all(own, "row", split_axis=0, concat_axis=0, tiled=True)
    sent_whole = take_tiles(integrals, place, virt_irrep, tile_map, 0, whole, 0, True)
    mirrored, sent_whole = lax.optimization_barrier((mirrored, sent_whole))
    part = antisymmetrize(own, mirrored, place, BODY_ROWS)
    part, sent_whole, place = lax.optimization_barrier((part, sent_whole, place))
    gathered = lax.all_gather(part, ("col", "depth"), axis=0, tiled=False)

    def exchange(offsets, tiles):
        moved = []
        for offset, tile in zip(offsets, tiles):
            if offset != (0, 0):
                moves = [(neighbour(r, offset, 1), r) for r in range(SIDE * SIDE)]
                tile = lax.ppermute(tile, "row", moves)
            moved.append(tile)
        return moved

    others = exchange(WHOLE, sent_whole)
    held = take_tiles(integrals, place, virt_irrep, tile_map, 0, whole, split, False)[0]
    held, place = lax.optimization_barrier((held, place))
    sent_split = take_tiles(integrals, place, virt_irrep, tile_map, whole, 0, split - 1, True)
    others[:EARLY], sent_split, place = lax.optimization_barrier((others[:EARLY], sent_split, place))
    kept_split = take_tiles(integrals, place, virt_irrep, tile_map, whole + split - 1, 0, 1, True)
    others = others + exchange(SPLIT[:-1], sent_split) + list(kept_split)
    held = subtract_tiles(held, others[:READY])
    result = contract(gathered, held, others[READY:], READY, BODY_ROWS)
    pieces = lax.all_to_all(result, "row", split_axis=0, concat_axis=0, tiled=True)
    return add_pieces(pieces, BODY_ROWS, own_rows - BODY_ROWS, own_cols)


def solution(mesh):
    placed = (P(("col", "depth"), "row", None), P("row", None, ("col", "depth")), P(), P())
    return jax.shard_map(
        local, mesh=mesh, in_specs=placed, out_specs=P("row", ("col", "depth")), check_vma=False
    )
```
